32 devices in a mesh: enc: 16 (over z, y, x), dec: 2 (over core).
Axes of the slice: x: 2, y: 2, z: 4, core: 2. Of those that a mesh axis runs over, the one named last changes fastest.
Arguments:
- pixels: bfloat16 [2, 144, 3072], P('dec', 'enc'), may hold values from -6 to 6
- tile_counts: int32 [2, 16], P('dec', 'enc'), may hold values from 1 to 9, as said below
- text_gaps: int32 [2, 16], P('dec', 'enc'), may hold values from 0 to 64
- stem_weight: bfloat16 [48, 384], replicated, may hold values from -0.875 to 0.875
- depth_weight: bfloat16 [49, 384], replicated, may hold values from -0.875 to 0.875
- norm_gain: float32 [384], replicated, may hold values from 0.5 to 2
- up_weight: bfloat16 [384, 768], replicated, may hold values from -0.3125 to 0.3125
- down_weight: bfloat16 [768, 384], replicated, may hold values from -0.21875 to 0.21875
- layer_scale: float32 [384], replicated, may hold values from 0.25 to 1
- embed_grad: bfloat16 [16, 416, 384], P('enc', 'dec'), may hold values from -6 to 6
Outputs:
- image_embeds: bfloat16 [16, 416, 384], P('enc', 'dec')
- stem_grad: float32 [48, 384], replicated
- depth_grad: float32 [49, 384], replicated
- gain_grad: float32 [384], replicated
- up_grad: float32 [384, 768], replicated
- down_grad: float32 [768, 384], replicated
- scale_grad: float32 [384], replicated
The draws below stay inside these ranges and needn't reach their ends.
Inputs may be any that keep to these rules, and one draw needn't show every extreme that they name: `tile_counts`: for each index of dec, the counts of each aligned group of four consecutive indices of enc sum to exactly 12.
All inputs are finite; a program needn't handle non-finite values.
Results may differ from the reference program's by a relative error of at most 0.013.
Values may be sent and summed in bfloat16 or wider, within the bound.
A program may use at most 64 MiB of HBM per device.

```python
import math
import jax
import jax.numpy as jnp
from jax import lax

WIDTH = 384
INNER = 768
KERNEL = 7
PATCH_CH = 48
TILE = 8
GAP = 64
MEAN_TILES = 3
SLOTS = 9
PIX = 3072
FEAT_TILE = 16
ENC_TILES = 144
SEQ = 416
N_ENC = 16
N_DEC = 2


def draw_tile_counts(key, part):
    key = jax.random.fold_in(key, 7)
    keys = jax.random.split(key, 5)
    group_total = N_ENC // 4
    forced = jax.random.randint(keys[0], (N_DEC, 1), 0, group_total)
    is_forced = jnp.arange(group_total)[None, :] == forced
    largest = jax.random.randint(keys[1], (N_DEC, group_total), MEAN_TILES, 3 * MEAN_TILES + 1)
    largest = jnp.where(is_forced, 3 * MEAN_TILES, largest)
    remainder = 4 * MEAN_TILES - largest
    first_part = jax.random.randint(keys[2], (N_DEC, group_total), 1, remainder - 1)
    first_part = jnp.where(is_forced, 1, first_part)
    second_part = jax.random.randint(keys[3], (N_DEC, group_total), 1, remainder - first_part)
    third_part = remainder - first_part - second_part
    grouped = jnp.stack([largest, first_part, second_part, third_part], axis=2)
    order_keys = jax.random.split(keys[4], N_DEC * group_total)
    orders = jax.vmap(lambda one_key: jax.random.permutation(one_key, 4))(order_keys).reshape(N_DEC, group_total, 4)
    mixed = jnp.take_along_axis(grouped, orders, axis=2)
    return mixed.reshape(N_DEC, N_ENC).astype(jnp.int32)


def set_ends(result, stream_key, low, high):
    longest = result.shape.index(max(result.shape))
    spots = []
    for shift in (0, 1):
        where = [jax.random.randint(jax.random.fold_in(stream_key, axis), (), 0, length) for axis, length in enumerate(result.shape)]
        where[longest] = (where[longest] + shift) % result.shape[longest]
        spots.append(tuple(where))
    return result.at[spots[0]].set(low).at[spots[1]].set(high)


def shard_levels(own_key, shape, pieces, least, high):
    loudness, own = 1.0, jax.random.fold_in(own_key, 6)
    for dim, blocks in pieces:
        draws = jnp.exp(jax.random.uniform(jax.random.fold_in(own, dim), (blocks,), jnp.float32, least / len(pieces), high / len(pieces)))
        loudness = loudness * jnp.repeat(draws, shape[dim] // blocks).reshape([-1 if axis == dim else 1 for axis in range(len(shape))])
    return loudness


def noise(stream_key, shape, width, limit, cuts=(), kind=jnp.bfloat16):
    gain = shard_levels(stream_key, shape, cuts, -0.22, 0.18) if cuts else 1.0
    drawn = jax.random.normal(stream_key, shape, jnp.float32) * width * gain
    return jnp.minimum(jnp.maximum(drawn, -limit), limit).astype(kind)


def setup_inputs(seed: int = 0) -> dict:
    streams_of = jax.random.split(jax.random.key(seed), 11)
    pixels = noise(streams_of[0], (N_DEC, ENC_TILES, PIX), 1.0, 6.0, ((0, 2), (1, 16)))
    tile_counts = draw_tile_counts(jax.random.fold_in(streams_of[10], 71), 0)
    text_gaps = set_ends(jax.random.randint(streams_of[2], (N_DEC, N_ENC), 0, GAP + 1), jax.random.fold_in(streams_of[2], 1), 0, GAP).astype(jnp.int32)
    stem_weight = noise(streams_of[3], (PATCH_CH, WIDTH), PATCH_CH ** -0.5, 0.875)
    depth_weight = noise(streams_of[4], (KERNEL * KERNEL, WIDTH), (KERNEL * KERNEL) ** -0.5, 0.875)
    norm_gain = jnp.clip(jnp.exp(jax.random.uniform(streams_of[5], (WIDTH,), jnp.float32, math.log(0.5), math.log(2.0))), 0.5, 2.0)
    up_weight = noise(streams_of[6], (WIDTH, INNER), WIDTH ** -0.5, 0.3125)
    down_weight = noise(streams_of[7], (INNER, WIDTH), INNER ** -0.5, 0.21875)
    layer_scale = jnp.clip(jnp.exp(jax.random.uniform(streams_of[8], (WIDTH,), jnp.float32, math.log(0.25), math.log(1.0))), 0.25, 1.0)
    embed_grad = noise(streams_of[9], (N_ENC, SEQ, WIDTH), 1.0, 6.0, ((0, 16), (1, 2)))
    return dict(pixels=pixels, tile_counts=tile_counts, text_gaps=text_gaps, stem_weight=stem_weight, depth_weight=depth_weight, norm_gain=norm_gain, up_weight=up_weight, down_weight=down_weight, layer_scale=layer_scale, embed_grad=embed_grad)


epsilon = 1e-06

def encode(tile_block, stem_weight, depth_weight, norm_gain, up_weight, down_weight, layer_scale):
    tile_total = tile_block.shape[0]
    reach = KERNEL // 2
    half_tile = TILE // 2
    patches = tile_block.reshape(tile_total * TILE * TILE, PATCH_CH)
    stem_out = jnp.dot(patches, stem_weight, preferred_element_type=jnp.float32).astype(jnp.bfloat16)
    stem_grid = stem_out.reshape(tile_total, TILE, TILE, WIDTH).astype(jnp.float32)
    padded = jnp.pad(stem_grid, ((0, 0), (reach, reach), (reach, reach), (0, 0)))
    kernel = depth_weight.astype(jnp.float32)
    mixed_field = jnp.zeros_like(stem_grid)
    for row_tap in range(KERNEL):
        for col_tap in range(KERNEL):
            mixed_field = mixed_field + padded[:, row_tap:row_tap + TILE, col_tap:col_tap + TILE, :] * kernel[row_tap * KERNEL + col_tap]
    flat_rows = mixed_field.reshape(-1, WIDTH)
    channel_mean = lax.optimization_barrier(jnp.mean(flat_rows, axis=1, keepdims=True))
    deviation = flat_rows - channel_mean
    variance = lax.optimization_barrier(jnp.mean(deviation * deviation, axis=1, keepdims=True))
    inv_std = lax.rsqrt(variance + epsilon)
    centred = deviation * inv_std
    normed = (centred * norm_gain).astype(jnp.bfloat16)
    hidden = jnp.dot(normed, up_weight, preferred_element_type=jnp.float32)
    activated = jax.nn.gelu(hidden).astype(jnp.bfloat16)
    projected = jnp.dot(activated, down_weight, preferred_element_type=jnp.float32)
    block_out = stem_grid.reshape(-1, WIDTH) + layer_scale * projected
    pooled = lax.optimization_barrier(jnp.mean(block_out.reshape(tile_total, half_tile, 2, half_tile, 2, WIDTH), axis=(2, 4)))
    pooled = pooled.reshape(tile_total, half_tile * half_tile, WIDTH)
    stored = (patches, padded, centred, inv_std, normed, hidden, activated, projected)
    return (pooled, stored)

def backward_head(stored, cotangent, down_weight, layer_scale):
    patches, padded, centred, inv_std, normed, hidden, activated, projected = stored
    tile_total = cotangent.shape[0]
    half_tile = TILE // 2
    spread_out = jnp.broadcast_to(cotangent.reshape(tile_total, half_tile, 1, half_tile, 1, WIDTH), (tile_total, half_tile, 2, half_tile, 2, WIDTH))
    grad_block = (0.25 * spread_out).reshape(-1, WIDTH)
    scale_term = lax.optimization_barrier(jnp.sum(grad_block * projected, axis=0))
    grad_proj = (grad_block * layer_scale).astype(jnp.bfloat16)
    down_term = lax.dot_general(activated, grad_proj, (((0,), (0,)), ((), ())), preferred_element_type=jnp.float32)
    grad_act = lax.dot_general(grad_proj, down_weight, (((1,), (1,)), ((), ())), preferred_element_type=jnp.float32)
    grad_hidden = jax.vjp(jax.nn.gelu, hidden)[1](grad_act)[0].astype(jnp.bfloat16)
    return (scale_term, down_term, grad_hidden, grad_block)

def backward_middle(stored, grad_hidden, up_weight, norm_gain):
    patches, padded, centred, inv_std, normed, hidden, activated, projected = stored
    up_term = lax.dot_general(normed, grad_hidden, (((0,), (0,)), ((), ())), preferred_element_type=jnp.float32)
    grad_normed = lax.dot_general(grad_hidden, up_weight, (((1,), (1,)), ((), ())), preferred_element_type=jnp.float32)
    gain_term = lax.optimization_barrier(jnp.sum(grad_normed * centred, axis=0))
    scaled = grad_normed * norm_gain
    grad_mixed = inv_std * (scaled - lax.optimization_barrier(jnp.mean(scaled, axis=1, keepdims=True)) - centred * lax.optimization_barrier(jnp.mean(scaled * centred, axis=1, keepdims=True)))
    return (gain_term, up_term, grad_mixed)

def backward_tail(stored, grad_mixed, grad_block, depth_weight):
    patches, padded, centred, inv_std, normed, hidden, activated, projected = stored
    tile_total = padded.shape[0]
    reach = KERNEL // 2
    grid_grad = grad_mixed.reshape(tile_total, TILE, TILE, WIDTH)
    grad_padded = jnp.pad(grid_grad, ((0, 0), (reach, reach), (reach, reach), (0, 0)))
    kernel = depth_weight.astype(jnp.float32)
    depth_rows = []
    inner = jnp.zeros_like(grid_grad)
    for row_tap in range(KERNEL):
        for col_tap in range(KERNEL):
            window = padded[:, row_tap:row_tap + TILE, col_tap:col_tap + TILE, :]
            depth_rows.append(lax.optimization_barrier(jnp.sum(window * grid_grad, axis=(0, 1, 2))))
            row_start = KERNEL - 1 - row_tap
            col_start = KERNEL - 1 - col_tap
            inner = inner + grad_padded[:, row_start:row_start + TILE, col_start:col_start + TILE, :] * kernel[row_tap * KERNEL + col_tap]
    depth_term = jnp.stack(depth_rows)
    grad_stem = (grad_block + inner.reshape(-1, WIDTH)).astype(jnp.bfloat16)
    stem_term = lax.dot_general(patches, grad_stem, (((0,), (0,)), ((), ())), preferred_element_type=jnp.float32)
    return (depth_term, stem_term)

def reference(pixels, tile_counts, text_gaps, stem_weight, depth_weight, norm_gain, up_weight, down_weight, layer_scale, embed_grad):
    owner_span = tile_counts * FEAT_TILE + text_gaps
    offsets = (jnp.cumsum(owner_span, axis=0) - owner_span + text_gaps).astype(jnp.int32)
    prefix = (jnp.cumsum(tile_counts, axis=1) - tile_counts).astype(jnp.int32)
    prefix_end = (prefix + tile_counts).astype(jnp.int32)
    tile_rank = jnp.arange(N_ENC * MEAN_TILES, dtype=jnp.int32)
    owner_index = lax.optimization_barrier(jnp.sum((prefix_end[:, None, :] <= tile_rank[None, :, None]).astype(jnp.int32), axis=2)).astype(jnp.int32)
    slot_index = (tile_rank[None, :] - jnp.take_along_axis(prefix, owner_index, axis=1)).astype(jnp.int32)
    source = (owner_index * SLOTS + slot_index).astype(jnp.int32)
    base_pos = jnp.take_along_axis(offsets, owner_index, axis=1) + slot_index * FEAT_TILE
    positions = (base_pos[:, :, None] + jnp.arange(FEAT_TILE, dtype=jnp.int32)[None, None, :]).astype(jnp.int32)

    def one_row(row_args):
        row_pixels, row_source, row_owner, row_positions = row_args
        tile_block = jnp.take(row_pixels, row_source, axis=0)
        pooled, stored = encode(tile_block, stem_weight, depth_weight, norm_gain, up_weight, down_weight, layer_scale)
        cotangent = embed_grad[row_owner[:, None], row_positions].astype(jnp.float32)
        scale_term, down_term, grad_hidden, grad_block = backward_head(stored, cotangent, down_weight, layer_scale)
        gain_term, up_term, grad_mixed = backward_middle(stored, grad_hidden, up_weight, norm_gain)
        depth_term, stem_term = backward_tail(stored, grad_mixed, grad_block, depth_weight)
        return (pooled.astype(jnp.bfloat16), (stem_term, depth_term, gain_term, up_term, down_term, scale_term))
    features, terms = lax.map(one_row, (pixels, source, owner_index, positions))
    owner_grid = jnp.broadcast_to(owner_index[:, :, None], positions.shape)
    image_embeds = jnp.zeros((N_ENC, SEQ, WIDTH), jnp.bfloat16).at[owner_grid, positions].set(features)
    grad_scale = 1.0 / math.sqrt(N_DEC * N_ENC * MEAN_TILES * FEAT_TILE)
    stem_grad = lax.optimization_barrier(jnp.sum(terms[0], axis=0)) * grad_scale
    depth_grad = lax.optimization_barrier(jnp.sum(terms[1], axis=0)) * grad_scale
    gain_grad = lax.optimization_barrier(jnp.sum(terms[2], axis=0)) * grad_scale
    up_grad = lax.optimization_barrier(jnp.sum(terms[3], axis=0)) * grad_scale
    down_grad = lax.optimization_barrier(jnp.sum(terms[4], axis=0)) * grad_scale
    scale_grad = lax.optimization_barrier(jnp.sum(terms[5], axis=0)) * grad_scale
    return (image_embeds, stem_grad, depth_grad, gain_grad, up_grad, down_grad, scale_grad)
```

```python
import functools
import math

import jax
import jax.numpy as jnp
from jax import lax
from jax.experimental import pallas as pl
from jax.experimental.pallas import tpu as pltpu
from jax.sharding import PartitionSpec as P

WIDTH = 384
INNER = 768
KERNEL = 7
REACH = 3
PATCH_CH = 48
TILE = 8
MEAN_TILES = 3
FEAT_TILE = 16
LANES = 128
GROUPS = WIDTH // LANES
EPSILON = 1e-06
GELU_A = math.sqrt(2.0 / math.pi)
GELU_B = 0.044715
MESH = pl.DeviceIdType.MESH

UP_AT = 0
DOWN_AT = UP_AT + (INNER // LANES) * WIDTH
STEM_AT = DOWN_AT + GROUPS * INNER
SMALL_AT = STEM_AT + GROUPS * PATCH_CH
SMALL = 64
PACKED = SMALL_AT + GROUPS * SMALL
GAIN_ROW = 56
SCALE_ROW = 57

NT = (((1,), (1,)), ((), ()))
TN = (((0,), (0,)), ((), ()))


def dot(left, right, dims=(((1,), (0,)), ((), ()))):
    return lax.dot_general(left, right, dims, preferred_element_type=jnp.float32)


def vmem():
    return pl.BlockSpec(memory_space=pltpu.VMEM)


def gather_kernel(n_dec, grad_ref, count_ref, gap_ref, full_ref, meta_ref, info, sends, recvs):
    enc_here = lax.axis_index("enc")
    dec_here = lax.axis_index("dec")
    seq_rows = grad_ref.shape[1]
    count = count_ref[0, 0]
    gap = gap_ref[0, 0]
    barrier = pltpu.get_barrier_semaphore()
    for step in range(1, n_dec):
        peer = lax.rem(dec_here + step, n_dec)
        pl.semaphore_signal(barrier, inc=1, device_id=(enc_here, peer), device_id_type=MESH)
    mine = pl.ds(pl.multiple_of(dec_here * 16, 16), 16)
    info[mine, :] = jnp.concatenate(
        [jnp.full((8, LANES), count, jnp.int32), jnp.full((8, LANES), gap, jnp.int32)], axis=0
    )
    pl.semaphore_wait(barrier, n_dec - 1)
    rows = pl.ds(pl.multiple_of(dec_here * seq_rows, 16), seq_rows)
    copies = []
    for step in range(1, n_dec):
        peer = lax.rem(dec_here + step, n_dec)
        for kind, (source, target) in enumerate(
            ((info.at[mine], info.at[mine]), (grad_ref.at[0], full_ref.at[rows]))
        ):
            copy = pltpu.make_async_remote_copy(
                src_ref=source,
                dst_ref=target,
                send_sem=sends.at[step - 1, kind],
                recv_sem=recvs.at[step - 1, kind],
                device_id=(enc_here, peer),
                device_id_type=MESH,
            )
            copy.start()
            copies.append(copy)
    full_ref[rows, :] = grad_ref[0]
    for copy in copies:
        copy.wait()
    start = jnp.full((8, LANES), gap, jnp.int32)
    for other in range(n_dec):
        span = info[other * 16 : other * 16 + 8, :] * FEAT_TILE + info[
            other * 16 + 8 : other * 16 + 16, :
        ]
        start = start + jnp.where(other < dec_here, span, 0)
    meta_ref[0:8, :] = start
    meta_ref[8:16, :] = jnp.full((8, LANES), count, jnp.int32)


def gather(n_dec, grad, counts, gaps):
    seq_rows = grad.shape[1]
    steps = max(n_dec - 1, 1)
    return pl.pallas_call(
        functools.partial(gather_kernel, n_dec),
        out_shape=(
            jax.ShapeDtypeStruct((n_dec * seq_rows, WIDTH), jnp.bfloat16),
            jax.ShapeDtypeStruct((16, LANES), jnp.int32),
        ),
        in_specs=[
            vmem(),
            pl.BlockSpec(memory_space=pltpu.SMEM),
            pl.BlockSpec(memory_space=pltpu.SMEM),
        ],
        out_specs=(vmem(), vmem()),
        scratch_shapes=[
            pltpu.VMEM((n_dec * 16, LANES), jnp.int32),
            pltpu.SemaphoreType.DMA((steps, 2)),
            pltpu.SemaphoreType.DMA((steps, 2)),
        ],
        compiler_params=pltpu.CompilerParams(collective_id=0, has_side_effects=True),
        name="gather_dec",
    )(grad, counts, gaps)


def shift_rows(value, amount):
    if amount == 0:
        return value
    row = lax.broadcasted_iota(jnp.int32, value.shape, 0)
    inside = (row + amount >= 0) & (row + amount < TILE)
    return jnp.where(inside, pltpu.roll(value, (-amount) % TILE, 0), 0.0)


def tower_kernel(
    tiles,
    pixels_ref,
    meta_ref,
    grad_ref,
    stem_ref,
    depth_ref,
    gain_ref,
    up_ref,
    down_ref,
    layer_ref,
    place_ref,
    pack_ref,
    wide,
    rows_in,
    stem_out,
    field,
    taps,
    normed_all,
    act_all,
    proj_all,
    hid_all,
    block_all,
    pool,
    depth_acc,
    small_acc,
):
    span = tiles * TILE
    chunk = 2 * span
    seq = grad_ref.shape[0]
    start = meta_ref[0:1, 0:1]
    count = meta_ref[8:9, 0:1]

    wide[...] = jnp.zeros_like(wide)
    for col in range(TILE):
        wide[col * PATCH_CH : (col + 1) * PATCH_CH, col * WIDTH : (col + 1) * WIDTH] = stem_ref[...]
    for tap in range(KERNEL * KERNEL):
        taps[tap * 8 : tap * 8 + 8, :] = jnp.broadcast_to(
            depth_ref[tap : tap + 1, :].astype(jnp.float32), (8, WIDTH)
        )
    depth_acc[...] = jnp.zeros_like(depth_acc)
    small_acc[...] = jnp.zeros_like(small_acc)
    pix = pixels_ref[...].astype(jnp.float32)
    for tile in range(tiles):
        rows_in[tile * 8 : tile * 8 + 8, :] = jnp.concatenate(
            [pix[tile : tile + 1, r * WIDTH : (r + 1) * WIDTH] for r in range(TILE)], axis=0
        )
    rows = rows_in[...].astype(jnp.bfloat16)
    for col in range(TILE):
        stem_out[col * span : (col + 1) * span, :] = (
            dot(rows, wide[:, col * WIDTH : (col + 1) * WIDTH])
            .astype(jnp.bfloat16)
            .astype(jnp.float32)
        )

    def at(col, tile):
        return pl.ds(pl.multiple_of(col * span + tile * 8, 8), 8)

    def mix(tile, carry):
        for group in range(GROUPS):
            lanes = slice(group * LANES, (group + 1) * LANES)
            source = [stem_out[at(col, tile), lanes] for col in range(TILE)]
            total = [jnp.zeros((8, LANES), jnp.float32)] * TILE
            for a in range(KERNEL):
                moved = [shift_rows(value, a - REACH) for value in source]
                for b in range(KERNEL):
                    tap = a * KERNEL + b
                    weight = taps[tap * 8 : tap * 8 + 8, lanes]
                    for col in range(TILE):
                        other = col + b - REACH
                        if 0 <= other < TILE:
                            total[col] = total[col] + moved[other] * weight
            for col in range(TILE):
                field[at(col, tile), lanes] = total[col]
        return carry

    lax.fori_loop(0, tiles, mix, 0)

    gain = gain_ref[...]
    layer = layer_ref[...]

    def fold(value):
        return jnp.sum(value.reshape(-1, 8, WIDTH), axis=0)

    def block(pair, carry):
        here = pl.ds(pl.multiple_of(pair * chunk, 16), chunk)
        mixed = field[here, :]
        dev = mixed - jnp.mean(mixed, axis=1, keepdims=True)
        inv = lax.rsqrt(jnp.mean(dev * dev, axis=1, keepdims=True) + EPSILON)
        centred = dev * inv
        normed = (centred * gain).astype(jnp.bfloat16)
        normed_all[here, :] = normed
        hidden = dot(normed, up_ref[...])
        square = hidden * hidden
        half = 0.5 + 0.5 * jnp.tanh(GELU_A * hidden * (1.0 + GELU_B * square))
        act = (hidden * half).astype(jnp.bfloat16)
        slope = half + hidden * (2.0 * half * (1.0 - half)) * (
            GELU_A + (3.0 * GELU_A * GELU_B) * square
        )
        act_all[here, :] = act
        projected = dot(act, down_ref[...])
        out = stem_out[here, :] + layer * projected
        both = out[:span] + out[span:]
        both = both + pltpu.roll(both, span - 1, 0)
        pool[pl.ds(pl.multiple_of(pair * span, 8), span), :] = 0.25 * both

        row = lax.broadcasted_iota(jnp.int32, (span, seq), 0)
        spot = lax.broadcasted_iota(jnp.int32, (span, seq), 1)
        tile = row // TILE
        want = start + tile * FEAT_TILE + (row % TILE) // 2 * 4 + pair
        pick = jnp.where((spot == want) & (tile < count), 0.25, 0.0).astype(jnp.bfloat16)
        once = dot(pick, grad_ref[...])
        grad_block = jnp.concatenate([once, once], axis=0)
        block_all[here, :] = grad_block
        small_acc[0:8, :] += fold(grad_block * projected)
        grad_proj = (grad_block * layer).astype(jnp.bfloat16)
        proj_all[here, :] = grad_proj
        grad_act = dot(grad_proj, down_ref[...], NT)
        grad_hidden = (grad_act * slope).astype(jnp.bfloat16)
        hid_all[here, :] = grad_hidden
        grad_normed = dot(grad_hidden, up_ref[...], NT)
        small_acc[8:16, :] += fold(grad_normed * centred)
        scaled = grad_normed * gain
        field[here, :] = inv * (
            scaled
            - jnp.mean(scaled, axis=1, keepdims=True)
            - centred * jnp.mean(scaled * centred, axis=1, keepdims=True)
        )
        return carry

    lax.fori_loop(0, TILE // 2, block, 0)

    place = jnp.zeros((seq, WIDTH), jnp.float32)
    for pair in range(TILE // 2):
        spot = lax.broadcasted_iota(jnp.int32, (seq, span), 0)
        row = lax.broadcasted_iota(jnp.int32, (seq, span), 1)
        tile = row // TILE
        want = start + tile * FEAT_TILE + (row % TILE) // 2 * 4 + pair
        hit = (spot == want) & (tile < count) & (row % 2 == 0)
        place = place + dot(
            jnp.where(hit, 1.0, 0.0).astype(jnp.bfloat16),
            pool[pair * span : (pair + 1) * span, :].astype(jnp.bfloat16),
        )
    place_ref[...] = place.astype(jnp.bfloat16)

    def pack(first, value):
        height = value.shape[0]
        for group in range(value.shape[1] // LANES):
            at_row = first + group * height
            pack_ref[at_row : at_row + height, :] = value[
                :, group * LANES : (group + 1) * LANES
            ].astype(jnp.bfloat16)

    pack(UP_AT, dot(normed_all[...], hid_all[...], TN))
    pack(DOWN_AT, dot(act_all[...], proj_all[...], TN))

    def unmix(tile, carry):
        for group in range(GROUPS):
            lanes = slice(group * LANES, (group + 1) * LANES)
            grads = [field[at(col, tile), lanes] for col in range(TILE)]
            source = [stem_out[at(col, tile), lanes] for col in range(TILE)]
            total = [block_all[at(col, tile), lanes] for col in range(TILE)]
            for a in range(KERNEL):
                moved = [shift_rows(value, REACH - a) for value in grads]
                for b in range(KERNEL):
                    tap = a * KERNEL + b
                    weight = taps[tap * 8 : tap * 8 + 8, lanes]
                    term = None
                    for col in range(TILE):
                        other = col - b + REACH
                        if 0 <= other < TILE:
                            total[col] = total[col] + moved[other] * weight
                            product = moved[other] * source[col]
                            term = product if term is None else term + product
                    depth_acc[tap * 8 : tap * 8 + 8, lanes] += term
            for col in range(TILE):
                block_all[at(col, tile), lanes] = total[col]
        return carry

    lax.fori_loop(0, tiles, unmix, 0)

    stem_term = jnp.zeros((PATCH_CH, WIDTH), jnp.float32)
    for col in range(TILE):
        grad_stem = block_all[col * span : (col + 1) * span, :].astype(jnp.bfloat16)
        stem_term = (
            stem_term + dot(rows, grad_stem, TN)[col * PATCH_CH : (col + 1) * PATCH_CH, :]
        )
    pack(STEM_AT, stem_term)
    taps_sum = jnp.sum(depth_acc[...].reshape(KERNEL * KERNEL, 8, WIDTH), axis=1)
    small = jnp.concatenate(
        [
            taps_sum,
            jnp.zeros((GAIN_ROW - KERNEL * KERNEL, WIDTH), jnp.float32),
            jnp.sum(small_acc[8:16, :], axis=0, keepdims=True),
            jnp.sum(small_acc[0:8, :], axis=0, keepdims=True),
            jnp.zeros((SMALL - SCALE_ROW - 1, WIDTH), jnp.float32),
        ],
        axis=0,
    )
    pack(SMALL_AT, small)
    if pack_ref.shape[0] > PACKED:
        pack_ref[PACKED:, :] = jnp.zeros((pack_ref.shape[0] - PACKED, LANES), jnp.bfloat16)


def tower(packed_rows, pixels, meta, grad, weights):
    tiles = pixels.shape[0]
    positions = tiles * TILE * TILE
    span = tiles * TILE
    stem_weight, depth_weight, norm_gain, up_weight, down_weight, layer_scale = weights
    f32, bf16 = jnp.float32, jnp.bfloat16
    return pl.pallas_call(
        functools.partial(tower_kernel, tiles),
        out_shape=(
            jax.ShapeDtypeStruct(grad.shape, bf16),
            jax.ShapeDtypeStruct((packed_rows, LANES), bf16),
        ),
        in_specs=[vmem()] * 9,
        out_specs=(vmem(), vmem()),
        scratch_shapes=[
            pltpu.VMEM((WIDTH, TILE * WIDTH), bf16),
            pltpu.VMEM((span, WIDTH), f32),
            pltpu.VMEM((positions, WIDTH), f32),
            pltpu.VMEM((positions, WIDTH), f32),
            pltpu.VMEM((KERNEL * KERNEL * 8, WIDTH), f32),
            pltpu.VMEM((positions, WIDTH), bf16),
            pltpu.VMEM((positions, INNER), bf16),
            pltpu.VMEM((positions, WIDTH), bf16),
            pltpu.VMEM((positions, INNER), bf16),
            pltpu.VMEM((positions, WIDTH), f32),
            pltpu.VMEM((positions // 2, WIDTH), f32),
            pltpu.VMEM((KERNEL * KERNEL * 8, WIDTH), f32),
            pltpu.VMEM((16, WIDTH), f32),
        ],
        compiler_params=pltpu.CompilerParams(vmem_limit_bytes=48 * 2**20),
        name="tower",
    )(
        pixels,
        meta,
        grad,
        stem_weight,
        depth_weight,
        norm_gain.reshape(1, WIDTH),
        up_weight,
        down_weight,
        layer_scale.reshape(1, WIDTH),
    )


def enc_factors(n_enc):
    if n_enc == 16:
        sizes = [2, 2, 4]
    else:
        sizes, left = [], n_enc
        while left > 1:
            size = next((s for s in (4, 2, 3, 5, 7) if left % s == 0), left)
            sizes.append(size)
            left //= size
    steps, stride = [], 1
    for size in sizes:
        steps.append((stride, size))
        stride *= size
    return steps


def reduce_kernel(n_enc, n_dec, scale, pack_ref, place_ref, *refs):
    factors = enc_factors(n_enc)
    sizes = [n_dec] + [size for _, size in factors]
    depth = len(sizes)
    seq_ref, stem_ref, depth_ref, gain_ref, up_ref, down_ref, scale_ref = refs[:7]
    held = refs[7 : 7 + depth]
    landed = refs[7 + depth : 7 + 2 * depth]
    full, place_in, place_send, place_recv, sum_send, sum_recv, out_send, out_recv = refs[
        7 + 2 * depth :
    ]
    enc_here = lax.axis_index("enc")
    dec_here = lax.axis_index("dec")
    odd = lax.rem(dec_here, 2)

    indices, peers = [dec_here], []
    peers.append([(enc_here, lax.rem(dec_here + s, n_dec)) for s in range(1, n_dec)])
    swap = len(factors) > 1 and factors[0][1] == factors[1][1]
    for place, (stride, size) in enumerate(factors):
        if swap and place < 2:
            other = factors[1 - place][0]
            stride = jnp.where(odd == 1, other, stride)
        index = lax.rem(lax.div(enc_here, stride), size)
        indices.append(index)
        peers.append(
            [
                (enc_here + (lax.rem(index + s, size) - index) * stride, dec_here)
                for s in range(1, size)
            ]
        )

    barrier = pltpu.get_barrier_semaphore()
    greeted = 0
    for group in peers:
        for peer in group:
            pl.semaphore_signal(barrier, inc=1, device_id=peer, device_id_type=MESH)
            greeted += 1
    pl.semaphore_wait(barrier, greeted)

    def send(source, target, send_sem, recv_sem, peer):
        copy = pltpu.make_async_remote_copy(
            src_ref=source,
            dst_ref=target,
            send_sem=send_sem,
            recv_sem=recv_sem,
            device_id=peer,
            device_id_type=MESH,
        )
        copy.start()
        return copy

    seq_rows = seq_ref.shape[1]
    waiting = []
    offset = 0
    offsets = []
    height = pack_ref.shape[0]
    sem = 0
    for stage in range(depth):
        size = sizes[stage]
        source = pack_ref if stage == 0 else held[stage - 1]
        part = height // size
        copies = []
        for step in range(1, size):
            index = lax.rem(indices[stage] + step, size)
            copies.append(
                send(
                    source.at[pl.ds(pl.multiple_of(index * part, 16), part)],
                    landed[stage].at[step - 1],
                    sum_send.at[sem],
                    sum_recv.at[sem],
                    peers[stage][step - 1],
                )
            )
            sem += 1
        if stage == 0:
            places = []
            for step in range(1, size):
                index = lax.rem(dec_here + step, size)
                places.append(
                    send(
                        place_ref.at[pl.ds(pl.multiple_of(index * seq_rows, 16), seq_rows)],
                        place_in.at[step - 1],
                        place_send.at[step - 1],
                        place_recv.at[step - 1],
                        peers[0][step - 1],
                    )
                )
        total = source[pl.ds(pl.multiple_of(indices[stage] * part, 16), part), :].astype(
            jnp.float32
        )
        for step, copy in enumerate(copies):
            copy.wait_recv()
            total = total + landed[stage][step].astype(jnp.float32)
        waiting += copies
        offset = offset + indices[stage] * part
        offsets.append(offset)
        height = part
        if stage < depth - 1:
            held[stage][...] = total.astype(jnp.bfloat16)
        else:
            full[pl.ds(pl.multiple_of(offset, 16), part), :] = total.astype(jnp.bfloat16)

    sem = 0
    for stage in reversed(range(depth)):
        mine = full.at[pl.ds(pl.multiple_of(offsets[stage], 16), height)]
        copies = []
        for step in range(1, sizes[stage]):
            copies.append(
                send(mine, mine, out_send.at[sem], out_recv.at[sem], peers[stage][step - 1])
            )
            sem += 1
        if stage == depth - 1:
            sequence = place_ref[
                pl.ds(pl.multiple_of(dec_here * seq_rows, 16), seq_rows), :
            ].astype(jnp.float32)
            for step, copy in enumerate(places):
                copy.wait_recv()
                sequence = sequence + place_in[step].astype(jnp.float32)
            seq_ref[0] = sequence.astype(jnp.bfloat16)
            waiting += places
        for copy in copies:
            copy.wait_recv()
        waiting += copies
        height *= sizes[stage]
    for copy in waiting:
        copy.wait_send()

    def unpack(first, rows, group):
        at_row = first + group * rows
        return full[at_row : at_row + rows, :].astype(jnp.float32) * scale

    for group in range(INNER // LANES):
        up_ref[:, group * LANES : (group + 1) * LANES] = unpack(UP_AT, WIDTH, group)
    for group in range(GROUPS):
        lanes = slice(group * LANES, (group + 1) * LANES)
        down_ref[:, lanes] = unpack(DOWN_AT, INNER, group)
        stem_ref[:, lanes] = unpack(STEM_AT, PATCH_CH, group)
        small = unpack(SMALL_AT, SMALL, group)
        depth_ref[:, lanes] = small[: KERNEL * KERNEL]
        gain_ref[:, lanes] = small[GAIN_ROW : GAIN_ROW + 1]
        scale_ref[:, lanes] = small[SCALE_ROW : SCALE_ROW + 1]


def reduce_all(n_enc, n_dec, scale, packed, place):
    sizes = [n_dec] + [size for _, size in enc_factors(n_enc)]
    rows = packed.shape[0]
    seq_rows = place.shape[0] // n_dec
    f32, bf16 = jnp.float32, jnp.bfloat16
    held, landed, height = [], [], rows
    for size in sizes:
        height //= size
        held.append(pltpu.VMEM((height, LANES), bf16))
        landed.append(pltpu.VMEM((max(size - 1, 1), height, LANES), bf16))
    steps = max(sum(size - 1 for size in sizes), 1)
    places = max(n_dec - 1, 1)
    return pl.pallas_call(
        functools.partial(reduce_kernel, n_enc, n_dec, scale),
        out_shape=(
            jax.ShapeDtypeStruct((1, seq_rows, WIDTH), bf16),
            jax.ShapeDtypeStruct((PATCH_CH, WIDTH), f32),
            jax.ShapeDtypeStruct((KERNEL * KERNEL, WIDTH), f32),
            jax.ShapeDtypeStruct((1, WIDTH), f32),
            jax.ShapeDtypeStruct((WIDTH, INNER), f32),
            jax.ShapeDtypeStruct((INNER, WIDTH), f32),
            jax.ShapeDtypeStruct((1, WIDTH), f32),
        ),
        in_specs=[vmem()] * 2,
        out_specs=(vmem(),) * 7,
        scratch_shapes=held
        + landed
        + [
            pltpu.VMEM((rows, LANES), bf16),
            pltpu.VMEM((places, seq_rows, WIDTH), bf16),
            pltpu.SemaphoreType.DMA((places,)),
            pltpu.SemaphoreType.DMA((places,)),
            pltpu.SemaphoreType.DMA((steps,)),
            pltpu.SemaphoreType.DMA((steps,)),
            pltpu.SemaphoreType.DMA((steps,)),
            pltpu.SemaphoreType.DMA((steps,)),
        ],
        compiler_params=pltpu.CompilerParams(
            collective_id=1, has_side_effects=True, vmem_limit_bytes=40 * 2**20
        ),
        name="reduce_all",
    )(packed, place)


def on_device(
    pixels,
    tile_counts,
    text_gaps,
    stem_weight,
    depth_weight,
    norm_gain,
    up_weight,
    down_weight,
    layer_scale,
    embed_grad,
):
    n_enc = lax.axis_size("enc")
    n_dec = lax.axis_size("dec")
    weights = (stem_weight, depth_weight, norm_gain, up_weight, down_weight, layer_scale)
    unit = n_enc * n_dec * 16
    packed_rows = -(-PACKED // unit) * unit
    grad, meta = gather(n_dec, embed_grad, tile_counts, text_gaps)
    place, packed = tower(packed_rows, pixels[0], meta, grad, weights)
    scale = 1.0 / math.sqrt(n_dec * n_enc * MEAN_TILES * FEAT_TILE)
    sequence, stem, depth, gain, up, down, layer = reduce_all(n_enc, n_dec, scale, packed, place)
    return (sequence, stem, depth, gain[0], up, down, layer[0])


def solution(mesh):
    return jax.shard_map(
        on_device,
        mesh=mesh,
        in_specs=(
            P("dec", "enc", None),
            P("dec", "enc"),
            P("dec", "enc"),
            P(),
            P(),
            P(),
            P(),
            P(),
            P(),
            P("enc", "dec", None),
        ),
        out_specs=(P("enc", "dec", None), P(), P(), P(), P(), P(), P()),
        check_vma=False,
    )
```

```python
import functools
import math

import jax
import jax.numpy as jnp
from jax import lax
from jax.experimental import pallas as pl
from jax.experimental.pallas import tpu as pltpu
from jax.sharding import PartitionSpec as P

WIDTH = 384
INNER = 768
KERNEL = 7
REACH = 3
PATCH_CH = 48
TILE = 8
MEAN_TILES = 3
FEAT_TILE = 16
LANES = 128
GROUPS = WIDTH // LANES
EPSILON = 1e-06
GELU_A = math.sqrt(2.0 / math.pi)
GELU_B = 0.044715
MESH = pl.DeviceIdType.MESH

UP_AT = 0
DOWN_AT = UP_AT + (INNER // LANES) * WIDTH
BIG = DOWN_AT + GROUPS * INNER
STEM_AT = 0
SMALL_AT = STEM_AT + GROUPS * PATCH_CH
SMALL = 64
LITTLE = SMALL_AT + GROUPS * SMALL
GAIN_ROW = 56
SCALE_ROW = 57
CHUNKS = 4

NT = (((1,), (1,)), ((), ()))
TN = (((0,), (0,)), ((), ()))


def dot(left, right, dims=(((1,), (0,)), ((), ()))):
    return lax.dot_general(left, right, dims, preferred_element_type=jnp.float32)


def vmem():
    return pl.BlockSpec(memory_space=pltpu.VMEM)


def whole_ref():
    return pl.BlockSpec(memory_space=pl.ANY)


def enc_digits(n_enc):
    sizes, left = ([2, 2, 4], 1) if n_enc == 16 else ([], n_enc)
    while left > 1:
        size = next((s for s in (4, 2, 3, 5, 7) if left % s == 0), left)
        sizes.append(size)
        left //= size
    digits, stride = [], 1
    for size in sizes:
        digits.append(("enc", stride, size))
        stride *= size
    return digits


def big_stages(n_enc, n_dec):
    digits = enc_digits(n_enc)
    return [s for s in [[("dec", 1, n_dec)], digits[:2], digits[2:]] if s]


def little_stages(n_enc, n_dec):
    digits = enc_digits(n_enc)
    return [s for s in [[("dec", 1, n_dec)] + digits[:2], digits[2:]] if s]


def stage_size(stage):
    return math.prod(size for _, _, size in stage)


def chunk_rows(n_enc, n_dec):
    unit = n_enc * n_dec * 16
    units = -(-BIG // unit)
    count = min(CHUNKS, units)
    return [unit * (units * (k + 1) // count - units * k // count) for k in range(count)]


class Route:
    def __init__(self, stage, enc_here, dec_here):
        here = {"enc": enc_here, "dec": dec_here}
        self.size = stage_size(stage)
        values = [lax.rem(lax.div(here[axis], stride), size) for axis, stride, size in stage]
        self.index, weight = 0, 1
        for value, (_, _, size) in zip(values, stage):
            self.index = self.index + value * weight
            weight *= size
        self.others, self.peers = [], []
        for step in range(1, self.size):
            other = lax.rem(self.index + step, self.size)
            self.others.append(other)
            place, left = dict(here), other
            for value, (axis, stride, size) in zip(values, stage):
                place[axis] = place[axis] + (lax.rem(left, size) - value) * stride
                left = lax.div(left, size)
            self.peers.append((place["enc"], place["dec"]))


def send(source, target, sems, number, peer):
    copy = pltpu.make_async_remote_copy(
        src_ref=source,
        dst_ref=target,
        send_sem=sems.at[number, 0],
        recv_sem=sems.at[number, 1],
        device_id=peer,
        device_id_type=MESH,
    )
    copy.start()
    return copy


class Sum:
    def __init__(self, routes, source, first, rows, target, landed, held, sems):
        self.routes, self.source, self.first, self.rows = routes, source, first, rows
        self.target, self.landed, self.held, self.sems = target, landed, held, sems
        self.number, self.at, self.height = 0, 0, rows
        self.offset, self.offsets, self.pending, self.sent = 0, [], [], []

    def done(self):
        return self.at > 2 * len(self.routes)

    def post(self, source, target, peer):
        copy = send(source, target, self.sems, self.number, peer)
        self.number += 1
        self.pending.append(copy)
        self.sent.append(copy)

    def advance(self):
        if self.done():
            return
        depth = len(self.routes)
        if 1 <= self.at <= depth:
            stage = self.at - 1
            route = self.routes[stage]
            part = self.height // route.size
            total = self.mine[
                pl.ds(pl.multiple_of(self.base + route.index * part, 16), part), :
            ].astype(jnp.float32)
            for step, copy in enumerate(self.pending):
                copy.wait_recv()
                total = total + self.landed[stage][step].astype(jnp.float32)
            self.offset = self.offset + route.index * part
            self.offsets.append(self.offset)
            self.height = part
            if stage < depth - 1:
                self.held[stage][...] = total.astype(jnp.bfloat16)
            else:
                rows = pl.ds(pl.multiple_of(self.first + self.offset, 16), part)
                self.target[rows, :] = total.astype(jnp.bfloat16)
        else:
            for copy in self.pending:
                copy.wait_recv()
            if self.at > depth:
                self.height *= self.routes[2 * depth - self.at].size
        self.pending = []
        if self.at < depth:
            route = self.routes[self.at]
            self.mine, self.base = (
                (self.source, self.first) if self.at == 0 else (self.held[self.at - 1], 0)
            )
            part = self.height // route.size
            for step, (other, peer) in enumerate(zip(route.others, route.peers)):
                rows = pl.ds(pl.multiple_of(self.base + other * part, 16), part)
                self.post(self.mine.at[rows], self.landed[self.at].at[step], peer)
        elif self.at < 2 * depth:
            stage = 2 * depth - 1 - self.at
            first = self.first + self.offsets[stage]
            rows = self.target.at[pl.ds(pl.multiple_of(first, 16), self.height)]
            for peer in self.routes[stage].peers:
                self.post(rows, rows, peer)
        self.at += 1

    def close(self):
        for copy in self.sent:
            copy.wait_send()


def sum_scratch(stages, rows):
    landed, held = [], []
    for stage in stages:
        size = stage_size(stage)
        rows //= size
        landed.append(pltpu.VMEM((max(size - 1, 1), rows, LANES), jnp.bfloat16))
        held.append(pltpu.VMEM((rows, LANES), jnp.bfloat16))
    steps = max(2 * sum(stage_size(stage) - 1 for stage in stages), 1)
    return landed + held + [pltpu.SemaphoreType.DMA((steps, 2))]


def shift_rows(value, amount):
    if amount == 0:
        return value
    row = lax.broadcasted_iota(jnp.int32, value.shape, 0)
    inside = (row + amount >= 0) & (row + amount < TILE)
    return jnp.where(inside, pltpu.roll(value, (-amount) % TILE, 0), 0.0)


def tower_kernel(n_enc, n_dec, tiles, *refs):
    (
        count_ref,
        gap_ref,
        pixels_any,
        stem_any,
        depth_any,
        gain_any,
        up_any,
        down_any,
        layer_any,
        grad_any,
        seq_ref,
        big_ref,
        little_ref,
        pixels_ref,
        stem_ref,
        depth_ref,
        gain_ref,
        up_ref,
        down_ref,
        layer_ref,
        grad_ref,
        info,
        load_sems,
        dec_sems,
        place_ref,
        place_in,
        big_pack,
        little_pack,
        wide,
        rows_in,
        stem_out,
        field,
        taps,
        normed_all,
        act_all,
        proj_all,
        hid_all,
        block_all,
        pool,
        depth_acc,
        small_acc,
    ) = refs[:41]
    spare = list(refs[41:])
    enc_here = lax.axis_index("enc")
    dec_here = lax.axis_index("dec")
    span = tiles * TILE
    chunk = 2 * span
    seq = grad_ref.shape[0]
    seq_rows = seq // n_dec

    big = [Route(stage, enc_here, dec_here) for stage in big_stages(n_enc, n_dec)]
    little = [Route(stage, enc_here, dec_here) for stage in little_stages(n_enc, n_dec)]
    across = Route([("dec", 1, n_dec)], enc_here, dec_here)

    def take(routes, *rest):
        depth = len(routes)
        landed, held, sems = spare[:depth], spare[depth : 2 * depth], spare[2 * depth]
        del spare[: 2 * depth + 1]
        return Sum(routes, *rest, landed, held, sems)

    sums, ready, first = [], [], 0
    for rows in chunk_rows(n_enc, n_dec):
        sums.append(take(big, big_pack, first, rows, big_ref))
        first += rows
        ready.append(first)
    last = take(little, little_pack, 0, little_pack.shape[0], little_ref)

    barrier = pltpu.get_barrier_semaphore()
    greeted = 0
    for route in little:
        for peer in route.peers:
            pl.semaphore_signal(barrier, inc=1, device_id=peer, device_id_type=MESH)
            greeted += 1
    own_rows = pl.ds(pl.multiple_of(dec_here * seq_rows, 16), seq_rows)
    loads = []
    for number, (source, target) in enumerate(
        (
            (pixels_any.at[0], pixels_ref),
            (stem_any, stem_ref),
            (depth_any, depth_ref),
            (gain_any, gain_ref.at[0]),
            (layer_any, layer_ref.at[0]),
            (up_any, up_ref),
            (down_any, down_ref),
            (grad_any.at[0], grad_ref.at[own_rows]),
        )
    ):
        copy = pltpu.make_async_copy(source, target, load_sems.at[number])
        copy.start()
        loads.append(copy)

    count_here = count_ref[0, 0]
    gap_here = gap_ref[0, 0]
    mine = pl.ds(pl.multiple_of(dec_here * 16, 16), 16)
    info[mine, :] = jnp.concatenate(
        [jnp.full((8, LANES), count_here, jnp.int32), jnp.full((8, LANES), gap_here, jnp.int32)],
        axis=0,
    )
    wide[...] = jnp.zeros_like(wide)
    for copy in loads[:3]:
        copy.wait()
    for col in range(TILE):
        wide[col * PATCH_CH : (col + 1) * PATCH_CH, col * WIDTH : (col + 1) * WIDTH] = stem_ref[...]
    for tap in range(KERNEL * KERNEL):
        taps[tap * 8 : tap * 8 + 8, :] = jnp.broadcast_to(
            depth_ref[tap : tap + 1, :].astype(jnp.float32), (8, WIDTH)
        )
    depth_acc[...] = jnp.zeros_like(depth_acc)
    small_acc[...] = jnp.zeros_like(small_acc)
    pix = pixels_ref[...].astype(jnp.float32)
    for tile in range(tiles):
        rows_in[tile * 8 : tile * 8 + 8, :] = jnp.concatenate(
            [pix[tile : tile + 1, r * WIDTH : (r + 1) * WIDTH] for r in range(TILE)], axis=0
        )
    rows = rows_in[...].astype(jnp.bfloat16)
    for col in range(TILE):
        stem_out[col * span : (col + 1) * span, :] = (
            dot(rows, wide[:, col * WIDTH : (col + 1) * WIDTH])
            .astype(jnp.bfloat16)
            .astype(jnp.float32)
        )

    def at(col, tile):
        return pl.ds(pl.multiple_of(col * span + tile * 8, 8), 8)

    def mix(tile, carry):
        for group in range(GROUPS):
            lanes = slice(group * LANES, (group + 1) * LANES)
            source = [stem_out[at(col, tile), lanes] for col in range(TILE)]
            total = [jnp.zeros((8, LANES), jnp.float32)] * TILE
            for a in range(KERNEL):
                moved = [shift_rows(value, a - REACH) for value in source]
                for b in range(KERNEL):
                    tap = a * KERNEL + b
                    weight = taps[tap * 8 : tap * 8 + 8, lanes]
                    for col in range(TILE):
                        other = col + b - REACH
                        if 0 <= other < TILE:
                            total[col] = total[col] + moved[other] * weight
            for col in range(TILE):
                field[at(col, tile), lanes] = total[col]
        return carry

    part = tiles * 2 // 3
    lax.fori_loop(0, part, mix, 0)
    pl.semaphore_wait(barrier, greeted)
    copies = []
    for step, peer in enumerate(across.peers):
        copies.append(send(info.at[mine], info.at[mine], dec_sems, 3 * step, peer))
        copies.append(send(grad_any.at[0], grad_ref.at[own_rows], dec_sems, 3 * step + 1, peer))
    lax.fori_loop(part, tiles, mix, 0)
    for copy in loads[3:]:
        copy.wait()
    for copy in copies:
        copy.wait()

    start = jnp.full((8, LANES), gap_here, jnp.int32)
    for other in range(n_dec):
        gone = info[other * 16 : other * 16 + 8, :] * FEAT_TILE
        gone = gone + info[other * 16 + 8 : other * 16 + 16, :]
        start = start + jnp.where(other < dec_here, gone, 0)
    start = start[0:1, 0:1]
    count = info[mine, :][0:1, 0:1]
    gain = gain_ref[...]
    layer = layer_ref[...]

    def fold(value):
        return jnp.sum(value.reshape(-1, 8, WIDTH), axis=0)

    def block(pair, carry):
        here = pl.ds(pl.multiple_of(pair * chunk, 16), chunk)
        mixed = field[here, :]
        dev = mixed - jnp.mean(mixed, axis=1, keepdims=True)
        inv = lax.rsqrt(jnp.mean(dev * dev, axis=1, keepdims=True) + EPSILON)
        centred = dev * inv
        normed = (centred * gain).astype(jnp.bfloat16)
        normed_all[here, :] = normed
        hidden = dot(normed, up_ref[...])
        square = hidden * hidden
        half = 0.5 + 0.5 * jnp.tanh(GELU_A * hidden * (1.0 + GELU_B * square))
        act = (hidden * half).astype(jnp.bfloat16)
        slope = half + hidden * (2.0 * half * (1.0 - half)) * (
            GELU_A + (3.0 * GELU_A * GELU_B) * square
        )
        act_all[here, :] = act
        projected = dot(act, down_ref[...])
        out = stem_out[here, :] + layer * projected
        both = out[:span] + out[span:]
        both = both + pltpu.roll(both, span - 1, 0)
        pool[pl.ds(pl.multiple_of(pair * span, 8), span), :] = 0.25 * both

        row = lax.broadcasted_iota(jnp.int32, (span, seq), 0)
        spot = lax.broadcasted_iota(jnp.int32, (span, seq), 1)
        tile = row // TILE
        want = start + tile * FEAT_TILE + (row % TILE) // 2 * 4 + pair
        pick = jnp.where((spot == want) & (tile < count), 0.25, 0.0).astype(jnp.bfloat16)
        once = dot(pick, grad_ref[...])
        grad_block = jnp.concatenate([once, once], axis=0)
        block_all[here, :] = grad_block
        small_acc[0:8, :] += fold(grad_block * projected)
        grad_proj = (grad_block * layer).astype(jnp.bfloat16)
        proj_all[here, :] = grad_proj
        grad_act = dot(grad_proj, down_ref[...], NT)
        grad_hidden = (grad_act * slope).astype(jnp.bfloat16)
        hid_all[here, :] = grad_hidden
        grad_normed = dot(grad_hidden, up_ref[...], NT)
        small_acc[8:16, :] += fold(grad_normed * centred)
        scaled = grad_normed * gain
        field[here, :] = inv * (
            scaled
            - jnp.mean(scaled, axis=1, keepdims=True)
            - centred * jnp.mean(scaled * centred, axis=1, keepdims=True)
        )
        return carry

    lax.fori_loop(0, TILE // 2, block, 0)

    place = jnp.zeros((seq, WIDTH), jnp.float32)
    for pair in range(TILE // 2):
        spot = lax.broadcasted_iota(jnp.int32, (seq, span), 0)
        row = lax.broadcasted_iota(jnp.int32, (seq, span), 1)
        tile = row // TILE
        want = start + tile * FEAT_TILE + (row % TILE) // 2 * 4 + pair
        hit = (spot == want) & (tile < count) & (row % 2 == 0)
        place = place + dot(
            jnp.where(hit, 1.0, 0.0).astype(jnp.bfloat16),
            pool[pair * span : (pair + 1) * span, :].astype(jnp.bfloat16),
        )
    place_ref[...] = place.astype(jnp.bfloat16)

    places = []
    for step, (other, peer) in enumerate(zip(across.others, across.peers)):
        rows_to = pl.ds(pl.multiple_of(other * seq_rows, 16), seq_rows)
        places.append(send(place_ref.at[rows_to], place_in.at[step], dec_sems, 3 * step + 2, peer))

    def pack(target, first, value):
        height = value.shape[0]
        for group in range(value.shape[1] // LANES):
            at_row = first + group * height
            target[at_row : at_row + height, :] = value[
                :, group * LANES : (group + 1) * LANES
            ].astype(jnp.bfloat16)

    def advance(filled):
        for one, end in zip(sums, ready):
            if end <= filled or filled == BIG:
                one.advance()

    if big_pack.shape[0] > BIG:
        big_pack[BIG:, :] = jnp.zeros((big_pack.shape[0] - BIG, LANES), jnp.bfloat16)
    pack(big_pack, UP_AT, dot(normed_all[...], hid_all[...], TN))
    advance(DOWN_AT)
    pack(big_pack, DOWN_AT, dot(act_all[...], proj_all[...], TN))
    advance(BIG)

    def unmix(tile, carry):
        for group in range(GROUPS):
            lanes = slice(group * LANES, (group + 1) * LANES)
            grads = [field[at(col, tile), lanes] for col in range(TILE)]
            source = [stem_out[at(col, tile), lanes] for col in range(TILE)]
            total = [block_all[at(col, tile), lanes] for col in range(TILE)]
            for a in range(KERNEL):
                moved = [shift_rows(value, REACH - a) for value in grads]
                for b in range(KERNEL):
                    tap = a * KERNEL + b
                    weight = taps[tap * 8 : tap * 8 + 8, lanes]
                    term = None
                    for col in range(TILE):
                        other = col - b + REACH
                        if 0 <= other < TILE:
                            total[col] = total[col] + moved[other] * weight
                            product = moved[other] * source[col]
                            term = product if term is None else term + product
                    depth_acc[tap * 8 : tap * 8 + 8, lanes] += term
            for col in range(TILE):
                block_all[at(col, tile), lanes] = total[col]
        return carry

    for third in range(3):
        lax.fori_loop(tiles * third // 3, tiles * (third + 1) // 3, unmix, 0)
        advance(BIG)

    stem_term = jnp.zeros((PATCH_CH, WIDTH), jnp.float32)
    for col in range(TILE):
        grad_stem = block_all[col * span : (col + 1) * span, :].astype(jnp.bfloat16)
        stem_term = (
            stem_term + dot(rows, grad_stem, TN)[col * PATCH_CH : (col + 1) * PATCH_CH, :]
        )
    pack(little_pack, STEM_AT, stem_term)
    taps_sum = jnp.sum(depth_acc[...].reshape(KERNEL * KERNEL, 8, WIDTH), axis=1)
    small = jnp.concatenate(
        [
            taps_sum,
            jnp.zeros((GAIN_ROW - KERNEL * KERNEL, WIDTH), jnp.float32),
            jnp.sum(small_acc[8:16, :], axis=0, keepdims=True),
            jnp.sum(small_acc[0:8, :], axis=0, keepdims=True),
            jnp.zeros((SMALL - SCALE_ROW - 1, WIDTH), jnp.float32),
        ],
        axis=0,
    )
    pack(little_pack, SMALL_AT, small)
    if little_pack.shape[0] > LITTLE:
        little_pack[LITTLE:, :] = jnp.zeros((little_pack.shape[0] - LITTLE, LANES), jnp.bfloat16)
    last.advance()

    sequence = place_ref[own_rows, :].astype(jnp.float32)
    for step, copy in enumerate(places):
        copy.wait_recv()
        sequence = sequence + place_in[step].astype(jnp.float32)
    seq_ref[...] = sequence.astype(jnp.bfloat16)
    while not (last.done() and all(one.done() for one in sums)):
        for one in sums:
            one.advance()
        last.advance()
    for one in [*sums, last]:
        one.close()
    for copy in places:
        copy.wait_send()


def tower(n_enc, n_dec, args):
    pixels, grad = args[2], args[-1]
    tiles = pixels.shape[1]
    positions = tiles * TILE * TILE
    span = tiles * TILE
    seq_rows = grad.shape[1]
    seq = n_dec * seq_rows
    f32, bf16 = jnp.float32, jnp.bfloat16
    chunks = chunk_rows(n_enc, n_dec)
    big_rows = sum(chunks)
    unit = n_enc * n_dec * 16
    little_rows = -(-LITTLE // unit) * unit
    steps = max(n_dec - 1, 1)
    smem = pl.BlockSpec(memory_space=pltpu.SMEM)
    scratch = [
        pltpu.VMEM((tiles, TILE * TILE * PATCH_CH), bf16),
        pltpu.VMEM((PATCH_CH, WIDTH), bf16),
        pltpu.VMEM((KERNEL * KERNEL, WIDTH), bf16),
        pltpu.VMEM((1, WIDTH), f32),
        pltpu.VMEM((WIDTH, INNER), bf16),
        pltpu.VMEM((INNER, WIDTH), bf16),
        pltpu.VMEM((1, WIDTH), f32),
        pltpu.VMEM((seq, WIDTH), bf16),
        pltpu.VMEM((n_dec * 16, LANES), jnp.int32),
        pltpu.SemaphoreType.DMA((8,)),
        pltpu.SemaphoreType.DMA((3 * steps, 2)),
        pltpu.VMEM((seq, WIDTH), bf16),
        pltpu.VMEM((steps, seq_rows, WIDTH), bf16),
        pltpu.VMEM((big_rows, LANES), bf16),
        pltpu.VMEM((little_rows, LANES), bf16),
        pltpu.VMEM((WIDTH, TILE * WIDTH), bf16),
        pltpu.VMEM((span, WIDTH), f32),
        pltpu.VMEM((positions, WIDTH), f32),
        pltpu.VMEM((positions, WIDTH), f32),
        pltpu.VMEM((KERNEL * KERNEL * 8, WIDTH), f32),
        pltpu.VMEM((positions, WIDTH), bf16),
        pltpu.VMEM((positions, INNER), bf16),
        pltpu.VMEM((positions, WIDTH), bf16),
        pltpu.VMEM((positions, INNER), bf16),
        pltpu.VMEM((positions, WIDTH), f32),
        pltpu.VMEM((positions // 2, WIDTH), f32),
        pltpu.VMEM((KERNEL * KERNEL * 8, WIDTH), f32),
        pltpu.VMEM((16, WIDTH), f32),
    ]
    for rows in chunks:
        scratch += sum_scratch(big_stages(n_enc, n_dec), rows)
    scratch += sum_scratch(little_stages(n_enc, n_dec), little_rows)
    return pl.pallas_call(
        functools.partial(tower_kernel, n_enc, n_dec, tiles),
        out_shape=(
            jax.ShapeDtypeStruct((seq_rows, WIDTH), bf16),
            jax.ShapeDtypeStruct((big_rows, LANES), bf16),
            jax.ShapeDtypeStruct((little_rows, LANES), bf16),
        ),
        in_specs=[smem, smem] + [whole_ref()] * 8,
        out_specs=(vmem(),) * 3,
        scratch_shapes=scratch,
        compiler_params=pltpu.CompilerParams(
            collective_id=0, has_side_effects=True, vmem_limit_bytes=56 * 2**20
        ),
        name="tower",
    )(*args)


def unpack_kernel(scale, seq_in, big, little, *refs):
    outs, holds, sems = refs[:7], refs[7:14], refs[14]
    seq_ref, stem_ref, depth_ref, gain_ref, up_ref, down_ref, scale_ref = holds
    copies = []

    def store(number):
        source, target = holds[number], outs[number]
        if number == 0:
            target = target.at[0]
        if number in (3, 6):
            source = source.at[0]
        copy = pltpu.make_async_copy(source, target, sems.at[number])
        copy.start()
        copies.append(copy)

    def unpack(source, first, rows, group):
        at_row = first + group * rows
        return source[at_row : at_row + rows, :].astype(jnp.float32) * scale

    for group in range(INNER // LANES):
        up_ref[:, group * LANES : (group + 1) * LANES] = unpack(big, UP_AT, WIDTH, group)
    store(4)
    for group in range(GROUPS):
        down_ref[:, group * LANES : (group + 1) * LANES] = unpack(big, DOWN_AT, INNER, group)
    store(5)
    seq_ref[...] = seq_in[...]
    store(0)
    for group in range(GROUPS):
        lanes = slice(group * LANES, (group + 1) * LANES)
        stem_ref[:, lanes] = unpack(little, STEM_AT, PATCH_CH, group)
        small = unpack(little, SMALL_AT, SMALL, group)
        depth_ref[:, lanes] = small[: KERNEL * KERNEL]
        gain_ref[:, lanes] = small[GAIN_ROW : GAIN_ROW + 1]
        scale_ref[:, lanes] = small[SCALE_ROW : SCALE_ROW + 1]
    for number in (1, 2, 3, 6):
        store(number)
    for copy in copies:
        copy.wait()


def unpack_all(scale, sequence, big, little):
    f32, bf16 = jnp.float32, jnp.bfloat16
    seq_rows = sequence.shape[0]
    shapes = [
        ((1, seq_rows, WIDTH), bf16),
        ((PATCH_CH, WIDTH), f32),
        ((KERNEL * KERNEL, WIDTH), f32),
        ((WIDTH,), f32),
        ((WIDTH, INNER), f32),
        ((INNER, WIDTH), f32),
        ((WIDTH,), f32),
    ]
    held = [(seq_rows, WIDTH)] + [s if len(s) == 2 else (1, WIDTH) for s, _ in shapes[1:]]
    return pl.pallas_call(
        functools.partial(unpack_kernel, scale),
        out_shape=tuple(jax.ShapeDtypeStruct(s, kind) for s, kind in shapes),
        in_specs=[vmem()] * 3,
        out_specs=(whole_ref(),) * 7,
        scratch_shapes=[pltpu.VMEM(s, kind) for s, (_, kind) in zip(held, shapes)]
        + [pltpu.SemaphoreType.DMA((7,))],
        compiler_params=pltpu.CompilerParams(vmem_limit_bytes=32 * 2**20),
        name="unpack",
    )(sequence, big, little)


def on_device(
    pixels,
    tile_counts,
    text_gaps,
    stem_weight,
    depth_weight,
    norm_gain,
    up_weight,
    down_weight,
    layer_scale,
    embed_grad,
):
    n_enc = lax.axis_size("enc")
    n_dec = lax.axis_size("dec")
    weights = (stem_weight, depth_weight, norm_gain, up_weight, down_weight, layer_scale)
    sequence, big, little = tower(
        n_enc, n_dec, (tile_counts, text_gaps, pixels, *weights, embed_grad)
    )
    scale = 1.0 / math.sqrt(n_dec * n_enc * MEAN_TILES * FEAT_TILE)
    return unpack_all(scale, sequence, big, little)


def solution(mesh):
    return jax.shard_map(
        on_device,
        mesh=mesh,
        in_specs=(
            P("dec", "enc", None),
            P("dec", "enc"),
            P("dec", "enc"),
            P(),
            P(),
            P(),
            P(),
            P(),
            P(),
            P("enc", "dec", None),
        ),
        out_specs=(P("enc", "dec", None), P(), P(), P(), P(), P(), P()),
        check_vma=False,
    )
```

```python
import functools
import math

import jax
import jax.numpy as jnp
from jax import lax
from jax.experimental import pallas as pl
from jax.experimental.pallas import tpu as pltpu
from jax.sharding import PartitionSpec as P

WIDTH = 384
INNER = 768
KERNEL = 7
REACH = 3
PATCH_CH = 48
TILE = 8
MEAN_TILES = 3
FEAT_TILE = 16
LANES = 128
GROUPS = WIDTH // LANES
EPSILON = 1e-06
GELU_A = math.sqrt(2.0 / math.pi)
GELU_B = 0.044715
MESH = pl.DeviceIdType.MESH

UP_AT = 0
DOWN_AT = UP_AT + (INNER // LANES) * WIDTH
BIG = DOWN_AT + GROUPS * INNER
STEM_AT = 0
SMALL_AT = STEM_AT + GROUPS * PATCH_CH
SMALL = 64
LITTLE = SMALL_AT + GROUPS * SMALL
GAIN_ROW = 56
SCALE_ROW = 57
CHUNKS = 4

NT = (((1,), (1,)), ((), ()))
TN = (((0,), (0,)), ((), ()))


def dot(left, right, dims=(((1,), (0,)), ((), ()))):
    return lax.dot_general(left, right, dims, preferred_element_type=jnp.float32)


def whole_ref():
    return pl.BlockSpec(memory_space=pl.ANY)


def enc_digits(n_enc):
    sizes, left = ([2, 2, 4], 1) if n_enc == 16 else ([], n_enc)
    while left > 1:
        size = next((s for s in (4, 2, 3, 5, 7) if left % s == 0), left)
        sizes.append(size)
        left //= size
    digits, stride = [], 1
    for size in sizes:
        digits.append(("enc", stride, size))
        stride *= size
    return digits


def big_stages(n_enc, n_dec, odd=0):
    digits = enc_digits(n_enc)
    if len(digits) > 1 and digits[0][2] == digits[1][2]:
        (_, one, size), (_, two, _) = digits[:2]
        lead = one + (two - one) * odd
        digits[:2] = [("enc", lead, size), ("enc", one + two - lead, size)]
    return [[("dec", 1, n_dec)]] + [[digit] for digit in digits]


def little_stages(n_enc, n_dec):
    digits = enc_digits(n_enc)
    return [s for s in [[("dec", 1, n_dec)] + digits[:2], digits[2:]] if s]


def stage_size(stage):
    return math.prod(size for _, _, size in stage)


def chunk_rows(n_enc, n_dec):
    unit = n_enc * n_dec * 16
    units = -(-BIG // unit)
    count = min(CHUNKS, units)
    return [unit * (units * (k + 1) // count - units * k // count) for k in range(count)]


class Route:
    def __init__(self, stage, enc_here, dec_here):
        here = {"enc": enc_here, "dec": dec_here}
        self.size = stage_size(stage)
        values = [lax.rem(lax.div(here[axis], stride), size) for axis, stride, size in stage]
        self.index, weight = 0, 1
        for value, (_, _, size) in zip(values, stage):
            self.index = self.index + value * weight
            weight *= size
        self.others, self.peers = [], []
        for step in range(1, self.size):
            other = lax.rem(self.index + step, self.size)
            self.others.append(other)
            place, left = dict(here), other
            for value, (axis, stride, size) in zip(values, stage):
                place[axis] = place[axis] + (lax.rem(left, size) - value) * stride
                left = lax.div(left, size)
            self.peers.append((place["enc"], place["dec"]))


def send(source, target, sems, number, peer):
    copy = pltpu.make_async_remote_copy(
        src_ref=source,
        dst_ref=target,
        send_sem=sems.at[number, 0],
        recv_sem=sems.at[number, 1],
        device_id=peer,
        device_id_type=MESH,
    )
    copy.start()
    return copy


class Sum:
    def __init__(self, routes, source, first, rows, target, landed, held, sems):
        self.routes, self.source, self.first, self.rows = routes, source, first, rows
        self.target, self.landed, self.held, self.sems = target, landed, held, sems
        self.number, self.at, self.height = 0, 0, rows
        self.offset, self.offsets, self.pending, self.sent = 0, [], [], []

    def done(self):
        return self.at > 2 * len(self.routes)

    def post(self, source, target, peer):
        copy = send(source, target, self.sems, self.number, peer)
        self.number += 1
        self.pending.append(copy)
        self.sent.append(copy)

    def advance(self):
        if self.done():
            return
        depth = len(self.routes)
        if 1 <= self.at <= depth:
            stage = self.at - 1
            route = self.routes[stage]
            part = self.height // route.size
            total = self.mine[
                pl.ds(pl.multiple_of(self.base + route.index * part, 16), part), :
            ].astype(jnp.float32)
            for step, copy in enumerate(self.pending):
                copy.wait_recv()
                total = total + self.landed[stage][step].astype(jnp.float32)
            self.offset = self.offset + route.index * part
            self.offsets.append(self.offset)
            self.height = part
            if stage < depth - 1:
                self.held[stage][...] = total.astype(jnp.bfloat16)
            else:
                rows = pl.ds(pl.multiple_of(self.first + self.offset, 16), part)
                self.target[rows, :] = total.astype(jnp.bfloat16)
        else:
            for copy in self.pending:
                copy.wait_recv()
            if self.at > depth:
                self.height *= self.routes[2 * depth - self.at].size
        self.pending = []
        if self.at < depth:
            route = self.routes[self.at]
            self.mine, self.base = (
                (self.source, self.first) if self.at == 0 else (self.held[self.at - 1], 0)
            )
            part = self.height // route.size
            for step, (other, peer) in enumerate(zip(route.others, route.peers)):
                rows = pl.ds(pl.multiple_of(self.base + other * part, 16), part)
                self.post(self.mine.at[rows], self.landed[self.at].at[step], peer)
        elif self.at < 2 * depth:
            stage = 2 * depth - 1 - self.at
            first = self.first + self.offsets[stage]
            rows = self.target.at[pl.ds(pl.multiple_of(first, 16), self.height)]
            for peer in self.routes[stage].peers:
                self.post(rows, rows, peer)
        self.at += 1

    def close(self):
        for copy in self.sent:
            copy.wait_send()


def sum_scratch(stages, rows):
    landed, held = [], []
    for stage in stages:
        size = stage_size(stage)
        rows //= size
        landed.append(pltpu.VMEM((max(size - 1, 1), rows, LANES), jnp.bfloat16))
        held.append(pltpu.VMEM((rows, LANES), jnp.bfloat16))
    steps = max(2 * sum(stage_size(stage) - 1 for stage in stages), 1)
    return landed + held + [pltpu.SemaphoreType.DMA((steps, 2))]


def shift_rows(value, amount):
    if amount == 0:
        return value
    row = lax.broadcasted_iota(jnp.int32, value.shape, 0)
    inside = (row + amount >= 0) & (row + amount < TILE)
    return jnp.where(inside, pltpu.roll(value, (-amount) % TILE, 0), 0.0)


def tower_kernel(n_enc, n_dec, tiles, *refs):
    (
        count_ref,
        gap_ref,
        pixels_any,
        stem_any,
        depth_any,
        gain_any,
        up_any,
        down_any,
        layer_any,
        grad_any,
        seq_any,
        big_any,
        little_any,
        pixels_ref,
        stem_ref,
        depth_ref,
        gain_ref,
        up_ref,
        down_ref,
        layer_ref,
        grad_ref,
        info,
        load_sems,
        dec_sems,
        place_ref,
        place_in,
        big_pack,
        little_pack,
        wide,
        rows_in,
        stem_out,
        field,
        taps,
        normed_all,
        act_all,
        proj_all,
        hid_all,
        block_all,
        pool,
        depth_acc,
        small_acc,
        seq_ref,
        big_ref,
        little_ref,
        store_sems,
    ) = refs[:45]
    spare = list(refs[45:])
    enc_here = lax.axis_index("enc")
    dec_here = lax.axis_index("dec")
    span = tiles * TILE
    chunk = 2 * span
    seq = grad_ref.shape[0]
    seq_rows = seq // n_dec

    odd = lax.rem(dec_here, 2)
    big = [Route(stage, enc_here, dec_here) for stage in big_stages(n_enc, n_dec, odd)]
    little = [Route(stage, enc_here, dec_here) for stage in little_stages(n_enc, n_dec)]
    across = Route([("dec", 1, n_dec)], enc_here, dec_here)

    def take(routes, *rest):
        depth = len(routes)
        landed, held, sems = spare[:depth], spare[depth : 2 * depth], spare[2 * depth]
        del spare[: 2 * depth + 1]
        return Sum(routes, *rest, landed, held, sems)

    sums, ready, first = [], [], 0
    for rows in chunk_rows(n_enc, n_dec):
        sums.append(take(big, big_pack, first, rows, big_ref))
        first += rows
        ready.append(first)
    last = take(little, little_pack, 0, little_pack.shape[0], little_ref)

    barrier = pltpu.get_barrier_semaphore()
    greeted = 0
    for route in little:
        for peer in route.peers:
            pl.semaphore_signal(barrier, inc=1, device_id=peer, device_id_type=MESH)
            greeted += 1
    own_rows = pl.ds(pl.multiple_of(dec_here * seq_rows, 16), seq_rows)
    loads = []
    for number, (source, target) in enumerate(
        (
            (pixels_any.at[0], pixels_ref),
            (stem_any, stem_ref),
            (depth_any, depth_ref),
            (gain_any, gain_ref.at[0]),
            (layer_any, layer_ref.at[0]),
            (up_any, up_ref),
            (down_any, down_ref),
            (grad_any.at[0], grad_ref.at[own_rows]),
        )
    ):
        copy = pltpu.make_async_copy(source, target, load_sems.at[number])
        copy.start()
        loads.append(copy)

    count_here = count_ref[0, 0]
    gap_here = gap_ref[0, 0]
    mine = pl.ds(pl.multiple_of(dec_here * 16, 16), 16)
    info[mine, :] = jnp.concatenate(
        [jnp.full((8, LANES), count_here, jnp.int32), jnp.full((8, LANES), gap_here, jnp.int32)],
        axis=0,
    )
    wide[...] = jnp.zeros_like(wide)
    for copy in loads[:3]:
        copy.wait()
    for col in range(TILE):
        wide[col * PATCH_CH : (col + 1) * PATCH_CH, col * WIDTH : (col + 1) * WIDTH] = stem_ref[...]
    for tap in range(KERNEL * KERNEL):
        taps[tap * 8 : tap * 8 + 8, :] = jnp.broadcast_to(
            depth_ref[tap : tap + 1, :].astype(jnp.float32), (8, WIDTH)
        )
    depth_acc[...] = jnp.zeros_like(depth_acc)
    small_acc[...] = jnp.zeros_like(small_acc)
    pix = pixels_ref[...].astype(jnp.float32)
    for tile in range(tiles):
        rows_in[tile * 8 : tile * 8 + 8, :] = jnp.concatenate(
            [pix[tile : tile + 1, r * WIDTH : (r + 1) * WIDTH] for r in range(TILE)], axis=0
        )
    rows = rows_in[...].astype(jnp.bfloat16)
    for col in range(TILE):
        stem_out[col * span : (col + 1) * span, :] = (
            dot(rows, wide[:, col * WIDTH : (col + 1) * WIDTH])
            .astype(jnp.bfloat16)
            .astype(jnp.float32)
        )

    def at(col, tile):
        return pl.ds(pl.multiple_of(col * span + tile * 8, 8), 8)

    def mix(tile, carry):
        for group in range(GROUPS):
            lanes = slice(group * LANES, (group + 1) * LANES)
            source = [stem_out[at(col, tile), lanes] for col in range(TILE)]
            total = [jnp.zeros((8, LANES), jnp.float32)] * TILE
            for a in range(KERNEL):
                moved = [shift_rows(value, a - REACH) for value in source]
                for b in range(KERNEL):
                    tap = a * KERNEL + b
                    weight = taps[tap * 8 : tap * 8 + 8, lanes]
                    for col in range(TILE):
                        other = col + b - REACH
                        if 0 <= other < TILE:
                            total[col] = total[col] + moved[other] * weight
            for col in range(TILE):
                field[at(col, tile), lanes] = total[col]
        return carry

    part = tiles * 2 // 3
    lax.fori_loop(0, part, mix, 0)
    pl.semaphore_wait(barrier, greeted)
    copies = []
    for step, peer in enumerate(across.peers):
        copies.append(send(info.at[mine], info.at[mine], dec_sems, 3 * step, peer))
        copies.append(send(grad_any.at[0], grad_ref.at[own_rows], dec_sems, 3 * step + 1, peer))
    lax.fori_loop(part, tiles, mix, 0)
    for copy in loads[3:]:
        copy.wait()
    for copy in copies:
        copy.wait()

    start = jnp.full((8, LANES), gap_here, jnp.int32)
    for other in range(n_dec):
        gone = info[other * 16 : other * 16 + 8, :] * FEAT_TILE
        gone = gone + info[other * 16 + 8 : other * 16 + 16, :]
        start = start + jnp.where(other < dec_here, gone, 0)
    start = start[0:1, 0:1]
    count = info[mine, :][0:1, 0:1]
    gain = gain_ref[...]
    layer = layer_ref[...]

    def fold(value):
        return jnp.sum(value.reshape(-1, 8, WIDTH), axis=0)

    def block(pair, carry):
        here = pl.ds(pl.multiple_of(pair * chunk, 16), chunk)
        mixed = field[here, :]
        dev = mixed - jnp.mean(mixed, axis=1, keepdims=True)
        inv = lax.rsqrt(jnp.mean(dev * dev, axis=1, keepdims=True) + EPSILON)
        centred = dev * inv
        normed = (centred * gain).astype(jnp.bfloat16)
        normed_all[here, :] = normed
        hidden = dot(normed, up_ref[...])
        square = hidden * hidden
        half = 0.5 + 0.5 * jnp.tanh(GELU_A * hidden * (1.0 + GELU_B * square))
        act = (hidden * half).astype(jnp.bfloat16)
        slope = half + hidden * (2.0 * half * (1.0 - half)) * (
            GELU_A + (3.0 * GELU_A * GELU_B) * square
        )
        act_all[here, :] = act
        projected = dot(act, down_ref[...])
        out = stem_out[here, :] + layer * projected
        both = out[:span] + out[span:]
        both = both + pltpu.roll(both, span - 1, 0)
        pool[pl.ds(pl.multiple_of(pair * span, 8), span), :] = 0.25 * both

        row = lax.broadcasted_iota(jnp.int32, (span, seq), 0)
        spot = lax.broadcasted_iota(jnp.int32, (span, seq), 1)
        tile = row // TILE
        want = start + tile * FEAT_TILE + (row % TILE) // 2 * 4 + pair
        pick = jnp.where((spot == want) & (tile < count), 0.25, 0.0).astype(jnp.bfloat16)
        once = dot(pick, grad_ref[...])
        grad_block = jnp.concatenate([once, once], axis=0)
        block_all[here, :] = grad_block
        small_acc[0:8, :] += fold(grad_block * projected)
        grad_proj = (grad_block * layer).astype(jnp.bfloat16)
        proj_all[here, :] = grad_proj
        grad_act = dot(grad_proj, down_ref[...], NT)
        grad_hidden = (grad_act * slope).astype(jnp.bfloat16)
        hid_all[here, :] = grad_hidden
        grad_normed = dot(grad_hidden, up_ref[...], NT)
        small_acc[8:16, :] += fold(grad_normed * centred)
        scaled = grad_normed * gain
        field[here, :] = inv * (
            scaled
            - jnp.mean(scaled, axis=1, keepdims=True)
            - centred * jnp.mean(scaled * centred, axis=1, keepdims=True)
        )
        return carry

    lax.fori_loop(0, TILE // 2, block, 0)

    def pack(target, first, value):
        height = value.shape[0]
        for group in range(value.shape[1] // LANES):
            at_row = first + group * height
            target[at_row : at_row + height, :] = value[
                :, group * LANES : (group + 1) * LANES
            ].astype(jnp.bfloat16)

    def advance(filled):
        for one, end in zip(sums, ready):
            if end <= filled or filled == BIG:
                one.advance()

    if big_pack.shape[0] > BIG:
        big_pack[BIG:, :] = jnp.zeros((big_pack.shape[0] - BIG, LANES), jnp.bfloat16)
    pack(big_pack, UP_AT, dot(normed_all[...], hid_all[...], TN))
    advance(DOWN_AT)
    pack(big_pack, DOWN_AT, dot(act_all[...], proj_all[...], TN))
    advance(BIG)

    place = jnp.zeros((seq, WIDTH), jnp.float32)
    for pair in range(TILE // 2):
        spot = lax.broadcasted_iota(jnp.int32, (seq, span), 0)
        row = lax.broadcasted_iota(jnp.int32, (seq, span), 1)
        tile = row // TILE
        want = start + tile * FEAT_TILE + (row % TILE) // 2 * 4 + pair
        hit = (spot == want) & (tile < count) & (row % 2 == 0)
        place = place + dot(
            jnp.where(hit, 1.0, 0.0).astype(jnp.bfloat16),
            pool[pair * span : (pair + 1) * span, :].astype(jnp.bfloat16),
        )
    place_ref[...] = place.astype(jnp.bfloat16)

    places = []
    for step, (other, peer) in enumerate(zip(across.others, across.peers)):
        rows_to = pl.ds(pl.multiple_of(other * seq_rows, 16), seq_rows)
        places.append(send(place_ref.at[rows_to], place_in.at[step], dec_sems, 3 * step + 2, peer))

    def unmix(tile, carry):
        for group in range(GROUPS):
            lanes = slice(group * LANES, (group + 1) * LANES)
            grads = [field[at(col, tile), lanes] for col in range(TILE)]
            source = [stem_out[at(col, tile), lanes] for col in range(TILE)]
            total = [block_all[at(col, tile), lanes] for col in range(TILE)]
            for a in range(KERNEL):
                moved = [shift_rows(value, REACH - a) for value in grads]
                for b in range(KERNEL):
                    tap = a * KERNEL + b
                    weight = taps[tap * 8 : tap * 8 + 8, lanes]
                    term = None
                    for col in range(TILE):
                        other = col - b + REACH
                        if 0 <= other < TILE:
                            total[col] = total[col] + moved[other] * weight
                            product = moved[other] * source[col]
                            term = product if term is None else term + product
                    depth_acc[tap * 8 : tap * 8 + 8, lanes] += term
            for col in range(TILE):
                block_all[at(col, tile), lanes] = total[col]
        return carry

    for third in range(3):
        lax.fori_loop(tiles * third // 3, tiles * (third + 1) // 3, unmix, 0)
        advance(BIG)

    stem_term = jnp.zeros((PATCH_CH, WIDTH), jnp.float32)
    for col in range(TILE):
        grad_stem = block_all[col * span : (col + 1) * span, :].astype(jnp.bfloat16)
        stem_term = (
            stem_term + dot(rows, grad_stem, TN)[col * PATCH_CH : (col + 1) * PATCH_CH, :]
        )
    pack(little_pack, STEM_AT, stem_term)
    taps_sum = jnp.sum(depth_acc[...].reshape(KERNEL * KERNEL, 8, WIDTH), axis=1)
    small = jnp.concatenate(
        [
            taps_sum,
            jnp.zeros((GAIN_ROW - KERNEL * KERNEL, WIDTH), jnp.float32),
            jnp.sum(small_acc[8:16, :], axis=0, keepdims=True),
            jnp.sum(small_acc[0:8, :], axis=0, keepdims=True),
            jnp.zeros((SMALL - SCALE_ROW - 1, WIDTH), jnp.float32),
        ],
        axis=0,
    )
    pack(little_pack, SMALL_AT, small)
    if little_pack.shape[0] > LITTLE:
        little_pack[LITTLE:, :] = jnp.zeros((little_pack.shape[0] - LITTLE, LANES), jnp.bfloat16)
    last.advance()

    sequence = place_ref[own_rows, :].astype(jnp.float32)
    for step, copy in enumerate(places):
        copy.wait_recv()
        sequence = sequence + place_in[step].astype(jnp.float32)
    seq_ref[...] = sequence.astype(jnp.bfloat16)
    stores = []

    def store(source, target):
        copy = pltpu.make_async_copy(source, target, store_sems.at[len(stores)])
        copy.start()
        stores.append(copy)

    store(seq_ref, seq_any)
    while not (last.done() and all(one.done() for one in sums)):
        for one, end in zip(sums, ready):
            if not one.done():
                one.advance()
                if one.done():
                    rows = slice(one.first, end)
                    store(big_ref.at[rows], big_any.at[rows])
        if not last.done():
            last.advance()
            if last.done():
                store(little_ref, little_any)
    for one in [*sums, last]:
        one.close()
    for copy in stores:
        copy.wait()
    for copy in places:
        copy.wait_send()


def tower(n_enc, n_dec, args):
    pixels, grad = args[2], args[-1]
    tiles = pixels.shape[1]
    positions = tiles * TILE * TILE
    span = tiles * TILE
    seq_rows = grad.shape[1]
    seq = n_dec * seq_rows
    f32, bf16 = jnp.float32, jnp.bfloat16
    chunks = chunk_rows(n_enc, n_dec)
    big_rows = sum(chunks)
    unit = n_enc * n_dec * 16
    little_rows = -(-LITTLE // unit) * unit
    steps = max(n_dec - 1, 1)
    smem = pl.BlockSpec(memory_space=pltpu.SMEM)
    scratch = [
        pltpu.VMEM((tiles, TILE * TILE * PATCH_CH), bf16),
        pltpu.VMEM((PATCH_CH, WIDTH), bf16),
        pltpu.VMEM((KERNEL * KERNEL, WIDTH), bf16),
        pltpu.VMEM((1, WIDTH), f32),
        pltpu.VMEM((WIDTH, INNER), bf16),
        pltpu.VMEM((INNER, WIDTH), bf16),
        pltpu.VMEM((1, WIDTH), f32),
        pltpu.VMEM((seq, WIDTH), bf16),
        pltpu.VMEM((n_dec * 16, LANES), jnp.int32),
        pltpu.SemaphoreType.DMA((8,)),
        pltpu.SemaphoreType.DMA((3 * steps, 2)),
        pltpu.VMEM((seq, WIDTH), bf16),
        pltpu.VMEM((steps, seq_rows, WIDTH), bf16),
        pltpu.VMEM((big_rows, LANES), bf16),
        pltpu.VMEM((little_rows, LANES), bf16),
        pltpu.VMEM((WIDTH, TILE * WIDTH), bf16),
        pltpu.VMEM((span, WIDTH), f32),
        pltpu.VMEM((positions, WIDTH), f32),
        pltpu.VMEM((positions, WIDTH), f32),
        pltpu.VMEM((KERNEL * KERNEL * 8, WIDTH), f32),
        pltpu.VMEM((positions, WIDTH), bf16),
        pltpu.VMEM((positions, INNER), bf16),
        pltpu.VMEM((positions, WIDTH), bf16),
        pltpu.VMEM((positions, INNER), bf16),
        pltpu.VMEM((positions, WIDTH), f32),
        pltpu.VMEM((positions // 2, WIDTH), f32),
        pltpu.VMEM((KERNEL * KERNEL * 8, WIDTH), f32),
        pltpu.VMEM((16, WIDTH), f32),
        pltpu.VMEM((seq_rows, WIDTH), bf16),
        pltpu.VMEM((big_rows, LANES), bf16),
        pltpu.VMEM((little_rows, LANES), bf16),
        pltpu.SemaphoreType.DMA((len(chunks) + 2,)),
    ]
    for rows in chunks:
        scratch += sum_scratch(big_stages(n_enc, n_dec), rows)
    scratch += sum_scratch(little_stages(n_enc, n_dec), little_rows)
    return pl.pallas_call(
        functools.partial(tower_kernel, n_enc, n_dec, tiles),
        out_shape=(
            jax.ShapeDtypeStruct((seq_rows, WIDTH), bf16),
            jax.ShapeDtypeStruct((big_rows, LANES), bf16),
            jax.ShapeDtypeStruct((little_rows, LANES), bf16),
        ),
        in_specs=[smem, smem] + [whole_ref()] * 8,
        out_specs=(whole_ref(),) * 3,
        scratch_shapes=scratch,
        compiler_params=pltpu.CompilerParams(
            collective_id=0, has_side_effects=True, vmem_limit_bytes=56 * 2**20
        ),
        name="tower",
    )(*args)


def unpack_kernel(scale, seq_any, big_any, little_any, *refs):
    outs, holds, sems = refs[:7], refs[7:14], refs[14]
    big, little = refs[15:]
    seq_ref, stem_ref, depth_ref, gain_ref, up_ref, down_ref, scale_ref = holds
    copies, loads = [], []
    for number, (source, target) in enumerate(
        (
            (big_any.at[UP_AT:DOWN_AT], big.at[UP_AT:DOWN_AT]),
            (big_any.at[DOWN_AT:BIG], big.at[DOWN_AT:BIG]),
            (seq_any, seq_ref),
            (little_any, little),
        )
    ):
        copy = pltpu.make_async_copy(source, target, sems.at[7 + number])
        copy.start()
        loads.append(copy)

    def store(number):
        source, target = holds[number], outs[number]
        if number == 0:
            target = target.at[0]
        if number in (3, 6):
            source = source.at[0]
        copy = pltpu.make_async_copy(source, target, sems.at[number])
        copy.start()
        copies.append(copy)

    def unpack(source, first, rows, group):
        at_row = first + group * rows
        return source[at_row : at_row + rows, :].astype(jnp.float32) * scale

    loads[0].wait()
    for group in range(INNER // LANES):
        up_ref[:, group * LANES : (group + 1) * LANES] = unpack(big, UP_AT, WIDTH, group)
    store(4)
    loads[1].wait()
    for group in range(GROUPS):
        down_ref[:, group * LANES : (group + 1) * LANES] = unpack(big, DOWN_AT, INNER, group)
    store(5)
    loads[2].wait()
    store(0)
    loads[3].wait()
    for group in range(GROUPS):
        lanes = slice(group * LANES, (group + 1) * LANES)
        stem_ref[:, lanes] = unpack(little, STEM_AT, PATCH_CH, group)
        small = unpack(little, SMALL_AT, SMALL, group)
        depth_ref[:, lanes] = small[: KERNEL * KERNEL]
        gain_ref[:, lanes] = small[GAIN_ROW : GAIN_ROW + 1]
        scale_ref[:, lanes] = small[SCALE_ROW : SCALE_ROW + 1]
    for number in (1, 2, 3, 6):
        store(number)
    for copy in copies:
        copy.wait()


def unpack_all(scale, sequence, big, little):
    f32, bf16 = jnp.float32, jnp.bfloat16
    seq_rows = sequence.shape[0]
    shapes = [
        ((1, seq_rows, WIDTH), bf16),
        ((PATCH_CH, WIDTH), f32),
        ((KERNEL * KERNEL, WIDTH), f32),
        ((WIDTH,), f32),
        ((WIDTH, INNER), f32),
        ((INNER, WIDTH), f32),
        ((WIDTH,), f32),
    ]
    held = [(seq_rows, WIDTH)] + [s if len(s) == 2 else (1, WIDTH) for s, _ in shapes[1:]]
    return pl.pallas_call(
        functools.partial(unpack_kernel, scale),
        out_shape=tuple(jax.ShapeDtypeStruct(s, kind) for s, kind in shapes),
        in_specs=[pl.BlockSpec(memory_space=pltpu.HBM)] * 3,
        out_specs=(whole_ref(),) * 7,
        scratch_shapes=[pltpu.VMEM(s, kind) for s, (_, kind) in zip(held, shapes)]
        + [
            pltpu.SemaphoreType.DMA((11,)),
            pltpu.VMEM(big.shape, bf16),
            pltpu.VMEM(little.shape, bf16),
        ],
        compiler_params=pltpu.CompilerParams(vmem_limit_bytes=56 * 2**20),
        name="unpack",
    )(sequence, big, little)


def on_device(
    pixels,
    tile_counts,
    text_gaps,
    stem_weight,
    depth_weight,
    norm_gain,
    up_weight,
    down_weight,
    layer_scale,
    embed_grad,
):
    n_enc = lax.axis_size("enc")
    n_dec = lax.axis_size("dec")
    weights = (stem_weight, depth_weight, norm_gain, up_weight, down_weight, layer_scale)
    sequence, big, little = tower(
        n_enc, n_dec, (tile_counts, text_gaps, pixels, *weights, embed_grad)
    )
    scale = 1.0 / math.sqrt(n_dec * n_enc * MEAN_TILES * FEAT_TILE)
    return unpack_all(scale, sequence, big, little)


def solution(mesh):
    return jax.shard_map(
        on_device,
        mesh=mesh,
        in_specs=(
            P("dec", "enc", None),
            P("dec", "enc"),
            P("dec", "enc"),
            P(),
            P(),
            P(),
            P(),
            P(),
            P(),
            P("enc", "dec", None),
        ),
        out_specs=(P("enc", "dec", None), P(), P(), P(), P(), P(), P()),
        check_vma=False,
    )
```

```python
import functools
import math

import jax
import jax.numpy as jnp
from jax import lax
from jax.experimental import pallas as pl
from jax.experimental.pallas import tpu as pltpu
from jax.sharding import PartitionSpec as P

WIDTH = 384
INNER = 768
KERNEL = 7
REACH = 3
PATCH_CH = 48
TILE = 8
MEAN_TILES = 3
FEAT_TILE = 16
LANES = 128
GROUPS = WIDTH // LANES
EPSILON = 1e-06
GELU_A = math.sqrt(2.0 / math.pi)
GELU_B = 0.044715
MESH = pl.DeviceIdType.MESH

UP_AT = 0
DOWN_AT = UP_AT + (INNER // LANES) * WIDTH
BIG = DOWN_AT + GROUPS * INNER
STEM_AT = 0
SMALL_AT = STEM_AT + GROUPS * PATCH_CH
SMALL = 64
LITTLE = SMALL_AT + GROUPS * SMALL
GAIN_ROW = 56
SCALE_ROW = 57
CHUNKS = 4

NT = (((1,), (1,)), ((), ()))
TN = (((0,), (0,)), ((), ()))


def dot(left, right, dims=(((1,), (0,)), ((), ()))):
    return lax.dot_general(left, right, dims, preferred_element_type=jnp.float32)


def whole_ref():
    return pl.BlockSpec(memory_space=pl.ANY)


def enc_digits(n_enc):
    sizes, left = ([2, 2, 4], 1) if n_enc == 16 else ([], n_enc)
    while left > 1:
        size = next((s for s in (4, 2, 3, 5, 7) if left % s == 0), left)
        sizes.append(size)
        left //= size
    digits, stride = [], 1
    for size in sizes:
        digits.append(("enc", stride, size))
        stride *= size
    return digits


def big_stages(n_enc, n_dec, odd=0):
    digits = enc_digits(n_enc)
    if len(digits) > 1 and digits[0][2] == digits[1][2]:
        (_, one, size), (_, two, _) = digits[:2]
        lead = one + (two - one) * odd
        digits[:2] = [("enc", lead, size), ("enc", one + two - lead, size)]
    return [[("dec", 1, n_dec)]] + [[digit] for digit in digits]


def little_stages(n_enc, n_dec):
    digits = enc_digits(n_enc)
    return [s for s in [[("dec", 1, n_dec)] + digits[:2], digits[2:]] if s]


def stage_size(stage):
    return math.prod(size for _, _, size in stage)


def chunk_rows(n_enc, n_dec):
    unit = n_enc * n_dec * 16
    units = -(-BIG // unit)
    count = min(CHUNKS, units)
    return [unit * (units * (k + 1) // count - units * k // count) for k in range(count)]


class Route:
    def __init__(self, stage, enc_here, dec_here):
        here = {"enc": enc_here, "dec": dec_here}
        self.size = stage_size(stage)
        values = [lax.rem(lax.div(here[axis], stride), size) for axis, stride, size in stage]
        self.index, weight = 0, 1
        for value, (_, _, size) in zip(values, stage):
            self.index = self.index + value * weight
            weight *= size
        self.others, self.peers = [], []
        for step in range(1, self.size):
            other = lax.rem(self.index + step, self.size)
            self.others.append(other)
            place, left = dict(here), other
            for value, (axis, stride, size) in zip(values, stage):
                place[axis] = place[axis] + (lax.rem(left, size) - value) * stride
                left = lax.div(left, size)
            self.peers.append((place["enc"], place["dec"]))


def send(source, target, sems, number, peer):
    copy = pltpu.make_async_remote_copy(
        src_ref=source,
        dst_ref=target,
        send_sem=sems.at[number, 0],
        recv_sem=sems.at[number, 1],
        device_id=peer,
        device_id_type=MESH,
    )
    copy.start()
    return copy


class Sum:
    def __init__(self, routes, source, first, rows, target, landed, held, sems):
        self.routes, self.source, self.first, self.rows = routes, source, first, rows
        self.target, self.landed, self.held, self.sems = target, landed, held, sems
        self.number, self.at, self.height = 0, 0, rows
        self.offset, self.offsets, self.pending, self.sent = 0, [], [], []

    def done(self):
        return self.at > 2 * len(self.routes)

    def post(self, source, target, peer):
        copy = send(source, target, self.sems, self.number, peer)
        self.number += 1
        self.pending.append(copy)
        self.sent.append(copy)

    def advance(self):
        if self.done():
            return
        depth = len(self.routes)
        if 1 <= self.at <= depth:
            stage = self.at - 1
            route = self.routes[stage]
            part = self.height // route.size
            total = self.mine[
                pl.ds(pl.multiple_of(self.base + route.index * part, 16), part), :
            ].astype(jnp.float32)
            for step, copy in enumerate(self.pending):
                copy.wait_recv()
                total = total + self.landed[stage][step].astype(jnp.float32)
            self.offset = self.offset + route.index * part
            self.offsets.append(self.offset)
            self.height = part
            if stage < depth - 1:
                self.held[stage][...] = total.astype(jnp.bfloat16)
            else:
                rows = pl.ds(pl.multiple_of(self.first + self.offset, 16), part)
                self.target[rows, :] = total.astype(jnp.bfloat16)
        else:
            for copy in self.pending:
                copy.wait_recv()
            if self.at > depth:
                self.height *= self.routes[2 * depth - self.at].size
        self.pending = []
        if self.at < depth:
            route = self.routes[self.at]
            self.mine, self.base = (
                (self.source, self.first) if self.at == 0 else (self.held[self.at - 1], 0)
            )
            part = self.height // route.size
            for step, (other, peer) in enumerate(zip(route.others, route.peers)):
                rows = pl.ds(pl.multiple_of(self.base + other * part, 16), part)
                self.post(self.mine.at[rows], self.landed[self.at].at[step], peer)
        elif self.at < 2 * depth:
            stage = 2 * depth - 1 - self.at
            first = self.first + self.offsets[stage]
            rows = self.target.at[pl.ds(pl.multiple_of(first, 16), self.height)]
            for peer in self.routes[stage].peers:
                self.post(rows, rows, peer)
        self.at += 1

    def close(self):
        for copy in self.sent:
            copy.wait_send()


def sum_scratch(stages, rows):
    landed, held = [], []
    for stage in stages:
        size = stage_size(stage)
        rows //= size
        landed.append(pltpu.VMEM((max(size - 1, 1), rows, LANES), jnp.bfloat16))
        held.append(pltpu.VMEM((rows, LANES), jnp.bfloat16))
    steps = max(2 * sum(stage_size(stage) - 1 for stage in stages), 1)
    return landed + held + [pltpu.SemaphoreType.DMA((steps, 2))]


def shift_rows(value, amount):
    if amount == 0:
        return value
    row = lax.broadcasted_iota(jnp.int32, value.shape, 0)
    inside = (row + amount >= 0) & (row + amount < TILE)
    return jnp.where(inside, pltpu.roll(value, (-amount) % TILE, 0), 0.0)


def tower_kernel(n_enc, n_dec, tiles, *refs):
    (
        count_ref,
        gap_ref,
        pixels_any,
        stem_any,
        depth_any,
        gain_any,
        up_any,
        down_any,
        layer_any,
        grad_any,
        seq_any,
        big_any,
        little_any,
        pixels_ref,
        stem_ref,
        depth_ref,
        gain_ref,
        up_ref,
        down_ref,
        layer_ref,
        grad_ref,
        info,
        load_sems,
        dec_sems,
        place_ref,
        place_in,
        big_pack,
        little_pack,
        wide,
        rows_in,
        stem_out,
        field,
        taps,
        normed_all,
        act_all,
        proj_all,
        hid_all,
        block_all,
        pool,
        depth_acc,
        small_acc,
        seq_ref,
        big_ref,
        little_ref,
        store_sems,
    ) = refs[:45]
    spare = list(refs[45:])
    enc_here = lax.axis_index("enc")
    dec_here = lax.axis_index("dec")
    span = tiles * TILE
    chunk = 2 * span
    seq = grad_ref.shape[0]
    seq_rows = seq // n_dec

    odd = lax.rem(dec_here, 2)
    ways = [
        [Route(stage, enc_here, dec_here) for stage in big_stages(n_enc, n_dec, turn)]
        for turn in (odd, 1 - odd)
    ]
    little = [Route(stage, enc_here, dec_here) for stage in little_stages(n_enc, n_dec)]
    across = Route([("dec", 1, n_dec)], enc_here, dec_here)

    def take(routes, *rest):
        depth = len(routes)
        landed, held, sems = spare[:depth], spare[depth : 2 * depth], spare[2 * depth]
        del spare[: 2 * depth + 1]
        return Sum(routes, *rest, landed, held, sems)

    sums, ready, first = [], [], 0
    for number, rows in enumerate(chunk_rows(n_enc, n_dec)):
        sums.append(take(ways[number % 2], big_pack, first, rows, big_ref))
        first += rows
        ready.append(first)
    last = take(little, little_pack, 0, little_pack.shape[0], little_ref)

    barrier = pltpu.get_barrier_semaphore()
    greeted = 0
    for route in little:
        for peer in route.peers:
            pl.semaphore_signal(barrier, inc=1, device_id=peer, device_id_type=MESH)
            greeted += 1
    own_rows = pl.ds(pl.multiple_of(dec_here * seq_rows, 16), seq_rows)
    loads = []
    for number, (source, target) in enumerate(
        (
            (pixels_any.at[0], pixels_ref),
            (stem_any, stem_ref),
            (depth_any, depth_ref),
            (gain_any, gain_ref.at[0]),
            (layer_any, layer_ref.at[0]),
            (up_any, up_ref),
            (down_any, down_ref),
            (grad_any.at[0], grad_ref.at[own_rows]),
        )
    ):
        copy = pltpu.make_async_copy(source, target, load_sems.at[number])
        copy.start()
        loads.append(copy)

    count_here = count_ref[0, 0]
    gap_here = gap_ref[0, 0]
    mine = pl.ds(pl.multiple_of(dec_here * 16, 16), 16)
    info[mine, :] = jnp.concatenate(
        [jnp.full((8, LANES), count_here, jnp.int32), jnp.full((8, LANES), gap_here, jnp.int32)],
        axis=0,
    )
    wide[...] = jnp.zeros_like(wide)
    for copy in loads[:3]:
        copy.wait()
    for col in range(TILE):
        wide[col * PATCH_CH : (col + 1) * PATCH_CH, col * WIDTH : (col + 1) * WIDTH] = stem_ref[...]
    for tap in range(KERNEL * KERNEL):
        taps[tap * 8 : tap * 8 + 8, :] = jnp.broadcast_to(
            depth_ref[tap : tap + 1, :].astype(jnp.float32), (8, WIDTH)
        )
    depth_acc[...] = jnp.zeros_like(depth_acc)
    small_acc[...] = jnp.zeros_like(small_acc)
    pix = pixels_ref[...].astype(jnp.float32)
    for tile in range(tiles):
        rows_in[tile * 8 : tile * 8 + 8, :] = jnp.concatenate(
            [pix[tile : tile + 1, r * WIDTH : (r + 1) * WIDTH] for r in range(TILE)], axis=0
        )
    rows = rows_in[...].astype(jnp.bfloat16)
    for col in range(TILE):
        stem_out[col * span : (col + 1) * span, :] = (
            dot(rows, wide[:, col * WIDTH : (col + 1) * WIDTH])
            .astype(jnp.bfloat16)
            .astype(jnp.float32)
        )

    def at(col, tile):
        return pl.ds(pl.multiple_of(col * span + tile * 8, 8), 8)

    def mix(tile, carry):
        for group in range(GROUPS):
            lanes = slice(group * LANES, (group + 1) * LANES)
            source = [stem_out[at(col, tile), lanes] for col in range(TILE)]
            total = [jnp.zeros((8, LANES), jnp.float32)] * TILE
            for a in range(KERNEL):
                moved = [shift_rows(value, a - REACH) for value in source]
                for b in range(KERNEL):
                    tap = a * KERNEL + b
                    weight = taps[tap * 8 : tap * 8 + 8, lanes]
                    for col in range(TILE):
                        other = col + b - REACH
                        if 0 <= other < TILE:
                            total[col] = total[col] + moved[other] * weight
            for col in range(TILE):
                field[at(col, tile), lanes] = total[col]
        return carry

    part = tiles * 2 // 3
    lax.fori_loop(0, part, mix, 0)
    pl.semaphore_wait(barrier, greeted)
    copies = []
    for step, peer in enumerate(across.peers):
        copies.append(send(info.at[mine], info.at[mine], dec_sems, 3 * step, peer))
        copies.append(send(grad_any.at[0], grad_ref.at[own_rows], dec_sems, 3 * step + 1, peer))
    lax.fori_loop(part, tiles, mix, 0)
    for copy in loads[3:]:
        copy.wait()
    for copy in copies:
        copy.wait()

    start = jnp.full((8, LANES), gap_here, jnp.int32)
    for other in range(n_dec):
        gone = info[other * 16 : other * 16 + 8, :] * FEAT_TILE
        gone = gone + info[other * 16 + 8 : other * 16 + 16, :]
        start = start + jnp.where(other < dec_here, gone, 0)
    start = start[0:1, 0:1]
    count = info[mine, :][0:1, 0:1]
    gain = gain_ref[...]
    layer = layer_ref[...]

    def fold(value):
        return jnp.sum(value.reshape(-1, 8, WIDTH), axis=0)

    def block(pair, carry):
        here = pl.ds(pl.multiple_of(pair * chunk, 16), chunk)
        mixed = field[here, :]
        dev = mixed - jnp.mean(mixed, axis=1, keepdims=True)
        inv = lax.rsqrt(jnp.mean(dev * dev, axis=1, keepdims=True) + EPSILON)
        centred = dev * inv
        normed = (centred * gain).astype(jnp.bfloat16)
        normed_all[here, :] = normed
        hidden = dot(normed, up_ref[...])
        square = hidden * hidden
        half = 0.5 + 0.5 * jnp.tanh(GELU_A * hidden * (1.0 + GELU_B * square))
        act = (hidden * half).astype(jnp.bfloat16)
        slope = half + hidden * (2.0 * half * (1.0 - half)) * (
            GELU_A + (3.0 * GELU_A * GELU_B) * square
        )
        act_all[here, :] = act
        projected = dot(act, down_ref[...])
        out = stem_out[here, :] + layer * projected
        both = out[:span] + out[span:]
        both = both + pltpu.roll(both, span - 1, 0)
        pool[pl.ds(pl.multiple_of(pair * span, 8), span), :] = 0.25 * both

        row = lax.broadcasted_iota(jnp.int32, (span, seq), 0)
        spot = lax.broadcasted_iota(jnp.int32, (span, seq), 1)
        tile = row // TILE
        want = start + tile * FEAT_TILE + (row % TILE) // 2 * 4 + pair
        pick = jnp.where((spot == want) & (tile < count), 0.25, 0.0).astype(jnp.bfloat16)
        once = dot(pick, grad_ref[...])
        grad_block = jnp.concatenate([once, once], axis=0)
        block_all[here, :] = grad_block
        small_acc[0:8, :] += fold(grad_block * projected)
        grad_proj = (grad_block * layer).astype(jnp.bfloat16)
        proj_all[here, :] = grad_proj
        grad_act = dot(grad_proj, down_ref[...], NT)
        grad_hidden = (grad_act * slope).astype(jnp.bfloat16)
        hid_all[here, :] = grad_hidden
        grad_normed = dot(grad_hidden, up_ref[...], NT)
        small_acc[8:16, :] += fold(grad_normed * centred)
        scaled = grad_normed * gain
        field[here, :] = inv * (
            scaled
            - jnp.mean(scaled, axis=1, keepdims=True)
            - centred * jnp.mean(scaled * centred, axis=1, keepdims=True)
        )
        return carry

    lax.fori_loop(0, TILE // 2, block, 0)

    def pack(target, first, value):
        height = value.shape[0]
        for group in range(value.shape[1] // LANES):
            at_row = first + group * height
            target[at_row : at_row + height, :] = value[
                :, group * LANES : (group + 1) * LANES
            ].astype(jnp.bfloat16)

    def advance(filled):
        for one, end in zip(sums, ready):
            if end <= filled or filled == BIG:
                one.advance()

    if big_pack.shape[0] > BIG:
        big_pack[BIG:, :] = jnp.zeros((big_pack.shape[0] - BIG, LANES), jnp.bfloat16)
    pack(big_pack, UP_AT, dot(normed_all[...], hid_all[...], TN))
    advance(DOWN_AT)
    pack(big_pack, DOWN_AT, dot(act_all[...], proj_all[...], TN))
    advance(BIG)

    place = jnp.zeros((seq, WIDTH), jnp.float32)
    for pair in range(TILE // 2):
        spot = lax.broadcasted_iota(jnp.int32, (seq, span), 0)
        row = lax.broadcasted_iota(jnp.int32, (seq, span), 1)
        tile = row // TILE
        want = start + tile * FEAT_TILE + (row % TILE) // 2 * 4 + pair
        hit = (spot == want) & (tile < count) & (row % 2 == 0)
        place = place + dot(
            jnp.where(hit, 1.0, 0.0).astype(jnp.bfloat16),
            pool[pair * span : (pair + 1) * span, :].astype(jnp.bfloat16),
        )
    place_ref[...] = place.astype(jnp.bfloat16)

    places = []
    for step, (other, peer) in enumerate(zip(across.others, across.peers)):
        rows_to = pl.ds(pl.multiple_of(other * seq_rows, 16), seq_rows)
        places.append(send(place_ref.at[rows_to], place_in.at[step], dec_sems, 3 * step + 2, peer))

    def unmix(tile, carry):
        for group in range(GROUPS):
            lanes = slice(group * LANES, (group + 1) * LANES)
            grads = [field[at(col, tile), lanes] for col in range(TILE)]
            source = [stem_out[at(col, tile), lanes] for col in range(TILE)]
            total = [block_all[at(col, tile), lanes] for col in range(TILE)]
            for a in range(KERNEL):
                moved = [shift_rows(value, REACH - a) for value in grads]
                for b in range(KERNEL):
                    tap = a * KERNEL + b
                    weight = taps[tap * 8 : tap * 8 + 8, lanes]
                    term = None
                    for col in range(TILE):
                        other = col - b + REACH
                        if 0 <= other < TILE:
                            total[col] = total[col] + moved[other] * weight
                            product = moved[other] * source[col]
                            term = product if term is None else term + product
                    depth_acc[tap * 8 : tap * 8 + 8, lanes] += term
            for col in range(TILE):
                block_all[at(col, tile), lanes] = total[col]
        return carry

    for third in range(3):
        lax.fori_loop(tiles * third // 3, tiles * (third + 1) // 3, unmix, 0)
        advance(BIG)

    stem_term = jnp.zeros((PATCH_CH, WIDTH), jnp.float32)
    for col in range(TILE):
        grad_stem = block_all[col * span : (col + 1) * span, :].astype(jnp.bfloat16)
        stem_term = (
            stem_term + dot(rows, grad_stem, TN)[col * PATCH_CH : (col + 1) * PATCH_CH, :]
        )
    pack(little_pack, STEM_AT, stem_term)
    taps_sum = jnp.sum(depth_acc[...].reshape(KERNEL * KERNEL, 8, WIDTH), axis=1)
    small = jnp.concatenate(
        [
            taps_sum,
            jnp.zeros((GAIN_ROW - KERNEL * KERNEL, WIDTH), jnp.float32),
            jnp.sum(small_acc[8:16, :], axis=0, keepdims=True),
            jnp.sum(small_acc[0:8, :], axis=0, keepdims=True),
            jnp.zeros((SMALL - SCALE_ROW - 1, WIDTH), jnp.float32),
        ],
        axis=0,
    )
    pack(little_pack, SMALL_AT, small)
    if little_pack.shape[0] > LITTLE:
        little_pack[LITTLE:, :] = jnp.zeros((little_pack.shape[0] - LITTLE, LANES), jnp.bfloat16)
    last.advance()

    sequence = place_ref[own_rows, :].astype(jnp.float32)
    for step, copy in enumerate(places):
        copy.wait_recv()
        sequence = sequence + place_in[step].astype(jnp.float32)
    seq_ref[...] = sequence.astype(jnp.bfloat16)
    stores = []

    def store(source, target):
        copy = pltpu.make_async_copy(source, target, store_sems.at[len(stores)])
        copy.start()
        stores.append(copy)

    store(seq_ref, seq_any)
    while not (last.done() and all(one.done() for one in sums)):
        for one, end in zip(sums, ready):
            if not one.done():
                one.advance()
                if one.done():
                    rows = slice(one.first, end)
                    store(big_ref.at[rows], big_any.at[rows])
        if not last.done():
            last.advance()
            if last.done():
                store(little_ref, little_any)
    for one in [*sums, last]:
        one.close()
    for copy in stores:
        copy.wait()
    for copy in places:
        copy.wait_send()


def tower(n_enc, n_dec, args):
    pixels, grad = args[2], args[-1]
    tiles = pixels.shape[1]
    positions = tiles * TILE * TILE
    span = tiles * TILE
    seq_rows = grad.shape[1]
    seq = n_dec * seq_rows
    f32, bf16 = jnp.float32, jnp.bfloat16
    chunks = chunk_rows(n_enc, n_dec)
    big_rows = sum(chunks)
    unit = n_enc * n_dec * 16
    little_rows = -(-LITTLE // unit) * unit
    steps = max(n_dec - 1, 1)
    smem = pl.BlockSpec(memory_space=pltpu.SMEM)
    scratch = [
        pltpu.VMEM((tiles, TILE * TILE * PATCH_CH), bf16),
        pltpu.VMEM((PATCH_CH, WIDTH), bf16),
        pltpu.VMEM((KERNEL * KERNEL, WIDTH), bf16),
        pltpu.VMEM((1, WIDTH), f32),
        pltpu.VMEM((WIDTH, INNER), bf16),
        pltpu.VMEM((INNER, WIDTH), bf16),
        pltpu.VMEM((1, WIDTH), f32),
        pltpu.VMEM((seq, WIDTH), bf16),
        pltpu.VMEM((n_dec * 16, LANES), jnp.int32),
        pltpu.SemaphoreType.DMA((8,)),
        pltpu.SemaphoreType.DMA((3 * steps, 2)),
        pltpu.VMEM((seq, WIDTH), bf16),
        pltpu.VMEM((steps, seq_rows, WIDTH), bf16),
        pltpu.VMEM((big_rows, LANES), bf16),
        pltpu.VMEM((little_rows, LANES), bf16),
        pltpu.VMEM((WIDTH, TILE * WIDTH), bf16),
        pltpu.VMEM((span, WIDTH), f32),
        pltpu.VMEM((positions, WIDTH), f32),
        pltpu.VMEM((positions, WIDTH), f32),
        pltpu.VMEM((KERNEL * KERNEL * 8, WIDTH), f32),
        pltpu.VMEM((positions, WIDTH), bf16),
        pltpu.VMEM((positions, INNER), bf16),
        pltpu.VMEM((positions, WIDTH), bf16),
        pltpu.VMEM((positions, INNER), bf16),
        pltpu.VMEM((positions, WIDTH), f32),
        pltpu.VMEM((positions // 2, WIDTH), f32),
        pltpu.VMEM((KERNEL * KERNEL * 8, WIDTH), f32),
        pltpu.VMEM((16, WIDTH), f32),
        pltpu.VMEM((seq_rows, WIDTH), bf16),
        pltpu.VMEM((big_rows, LANES), bf16),
        pltpu.VMEM((little_rows, LANES), bf16),
        pltpu.SemaphoreType.DMA((len(chunks) + 2,)),
    ]
    for rows in chunks:
        scratch += sum_scratch(big_stages(n_enc, n_dec), rows)
    scratch += sum_scratch(little_stages(n_enc, n_dec), little_rows)
    return pl.pallas_call(
        functools.partial(tower_kernel, n_enc, n_dec, tiles),
        out_shape=(
            jax.ShapeDtypeStruct((seq_rows, WIDTH), bf16),
            jax.ShapeDtypeStruct((big_rows, LANES), bf16),
            jax.ShapeDtypeStruct((little_rows, LANES), bf16),
        ),
        in_specs=[smem, smem] + [whole_ref()] * 8,
        out_specs=(whole_ref(),) * 3,
        scratch_shapes=scratch,
        compiler_params=pltpu.CompilerParams(
            collective_id=0, has_side_effects=True, vmem_limit_bytes=56 * 2**20
        ),
        name="tower",
    )(*args)


def unpack_kernel(scale, seq_any, big_any, little_any, *refs):
    outs, holds, sems = refs[:7], refs[7:14], refs[14]
    big, little = refs[15:]
    seq_ref, stem_ref, depth_ref, gain_ref, up_ref, down_ref, scale_ref = holds
    strips = [(UP_AT + k * WIDTH, WIDTH, 4, k) for k in range(INNER // LANES)]
    strips += [(DOWN_AT + k * INNER, INNER, 5, k) for k in range(GROUPS)]
    count = [0]

    def move(source, target):
        copy = pltpu.make_async_copy(source, target, sems.at[count[0]])
        copy.start()
        count[0] += 1
        return copy

    loads = [
        move(big_any.at[first : first + rows], big.at[first : first + rows])
        for first, rows, _, _ in strips
    ]
    small_load = move(little_any, little)
    stores = [move(seq_any, outs[0].at[0])]

    def unpack(source, first, rows):
        return source[first : first + rows, :].astype(jnp.float32) * scale

    for load, (first, rows, number, group) in zip(loads, strips):
        lanes = slice(group * LANES, (group + 1) * LANES)
        load.wait()
        holds[number][:, lanes] = unpack(big, first, rows)
        stores.append(move(holds[number].at[:, lanes], outs[number].at[:, lanes]))
    small_load.wait()
    for group in range(GROUPS):
        lanes = slice(group * LANES, (group + 1) * LANES)
        stem_ref[:, lanes] = unpack(little, STEM_AT + group * PATCH_CH, PATCH_CH)
        small = unpack(little, SMALL_AT + group * SMALL, SMALL)
        depth_ref[:, lanes] = small[: KERNEL * KERNEL]
        gain_ref[:, lanes] = small[GAIN_ROW : GAIN_ROW + 1]
        scale_ref[:, lanes] = small[SCALE_ROW : SCALE_ROW + 1]
    for number in (1, 2):
        stores.append(move(holds[number], outs[number]))
    for number in (3, 6):
        stores.append(move(holds[number].at[0], outs[number]))
    for copy in stores:
        copy.wait()


def unpack_all(scale, sequence, big, little):
    f32, bf16 = jnp.float32, jnp.bfloat16
    seq_rows = sequence.shape[0]
    shapes = [
        ((1, seq_rows, WIDTH), bf16),
        ((PATCH_CH, WIDTH), f32),
        ((KERNEL * KERNEL, WIDTH), f32),
        ((WIDTH,), f32),
        ((WIDTH, INNER), f32),
        ((INNER, WIDTH), f32),
        ((WIDTH,), f32),
    ]
    held = [(seq_rows, WIDTH)] + [s if len(s) == 2 else (1, WIDTH) for s, _ in shapes[1:]]
    return pl.pallas_call(
        functools.partial(unpack_kernel, scale),
        out_shape=tuple(jax.ShapeDtypeStruct(s, kind) for s, kind in shapes),
        in_specs=[pl.BlockSpec(memory_space=pltpu.HBM)] * 3,
        out_specs=(whole_ref(),) * 7,
        scratch_shapes=[pltpu.VMEM(s, kind) for s, (_, kind) in zip(held, shapes)]
        + [
            pltpu.SemaphoreType.DMA((24,)),
            pltpu.VMEM(big.shape, bf16),
            pltpu.VMEM(little.shape, bf16),
        ],
        compiler_params=pltpu.CompilerParams(vmem_limit_bytes=56 * 2**20),
        name="unpack",
    )(sequence, big, little)


def on_device(
    pixels,
    tile_counts,
    text_gaps,
    stem_weight,
    depth_weight,
    norm_gain,
    up_weight,
    down_weight,
    layer_scale,
    embed_grad,
):
    n_enc = lax.axis_size("enc")
    n_dec = lax.axis_size("dec")
    weights = (stem_weight, depth_weight, norm_gain, up_weight, down_weight, layer_scale)
    sequence, big, little = tower(
        n_enc, n_dec, (tile_counts, text_gaps, pixels, *weights, embed_grad)
    )
    scale = 1.0 / math.sqrt(n_dec * n_enc * MEAN_TILES * FEAT_TILE)
    return unpack_all(scale, sequence, big, little)


def solution(mesh):
    return jax.shard_map(
        on_device,
        mesh=mesh,
        in_specs=(
            P("dec", "enc", None),
            P("dec", "enc"),
            P("dec", "enc"),
            P(),
            P(),
            P(),
            P(),
            P(),
            P(),
            P("enc", "dec", None),
        ),
        out_specs=(P("enc", "dec", None), P(), P(), P(), P(), P(), P()),
        check_vma=False,
    )
```

```python
import functools
import math

import jax
import jax.numpy as jnp
from jax import lax
from jax.experimental import pallas as pl
from jax.experimental.pallas import tpu as pltpu
from jax.sharding import PartitionSpec as P

WIDTH = 384
INNER = 768
KERNEL = 7
REACH = 3
PATCH_CH = 48
TILE = 8
MEAN_TILES = 3
FEAT_TILE = 16
LANES = 128
GROUPS = WIDTH // LANES
EPSILON = 1e-06
GELU_A = math.sqrt(2.0 / math.pi)
GELU_B = 0.044715
MESH = pl.DeviceIdType.MESH

UP_AT = 0
DOWN_AT = UP_AT + (INNER // LANES) * WIDTH
BIG = DOWN_AT + GROUPS * INNER
STEM_AT = 0
SMALL_AT = STEM_AT + GROUPS * PATCH_CH
SMALL = 64
LITTLE = SMALL_AT + GROUPS * SMALL
GAIN_ROW = 56
SCALE_ROW = 57
CHUNKS = 4

NT = (((1,), (1,)), ((), ()))
TN = (((0,), (0,)), ((), ()))


def dot(left, right, dims=(((1,), (0,)), ((), ()))):
    return lax.dot_general(left, right, dims, preferred_element_type=jnp.float32)


def whole_ref():
    return pl.BlockSpec(memory_space=pl.ANY)


def enc_digits(n_enc):
    sizes, left = ([2, 2, 4], 1) if n_enc == 16 else ([], n_enc)
    while left > 1:
        size = next((s for s in (4, 2, 3, 5, 7) if left % s == 0), left)
        sizes.append(size)
        left //= size
    digits, stride = [], 1
    for size in sizes:
        digits.append(("enc", stride, size))
        stride *= size
    return digits


def big_stages(n_enc, n_dec, odd=0):
    digits = enc_digits(n_enc)
    if len(digits) > 1 and digits[0][2] == digits[1][2]:
        (_, one, size), (_, two, _) = digits[:2]
        lead = one + (two - one) * odd
        digits[:2] = [("enc", lead, size), ("enc", one + two - lead, size)]
    return [[("dec", 1, n_dec)]] + [[digit] for digit in digits]


def little_stages(n_enc, n_dec):
    digits = enc_digits(n_enc)
    return [s for s in [[("dec", 1, n_dec)] + digits[:2], digits[2:]] if s]


def stage_size(stage):
    return math.prod(size for _, _, size in stage)


def chunk_rows(n_enc, n_dec):
    unit = n_enc * n_dec * 16
    units = -(-BIG // unit)
    count = min(CHUNKS, units)
    return [unit * (units * (k + 1) // count - units * k // count) for k in range(count)]


class Route:
    def __init__(self, stage, enc_here, dec_here):
        here = {"enc": enc_here, "dec": dec_here}
        self.size = stage_size(stage)
        values = [lax.rem(lax.div(here[axis], stride), size) for axis, stride, size in stage]
        self.index, weight = 0, 1
        for value, (_, _, size) in zip(values, stage):
            self.index = self.index + value * weight
            weight *= size
        self.others, self.peers = [], []
        for step in range(1, self.size):
            other = lax.rem(self.index + step, self.size)
            self.others.append(other)
            place, left = dict(here), other
            for value, (axis, stride, size) in zip(values, stage):
                place[axis] = place[axis] + (lax.rem(left, size) - value) * stride
                left = lax.div(left, size)
            self.peers.append((place["enc"], place["dec"]))


def send(source, target, sems, number, peer):
    copy = pltpu.make_async_remote_copy(
        src_ref=source,
        dst_ref=target,
        send_sem=sems.at[number, 0],
        recv_sem=sems.at[number, 1],
        device_id=peer,
        device_id_type=MESH,
    )
    copy.start()
    return copy


class Sum:
    def __init__(self, routes, source, first, rows, target, landed, held, sems):
        self.routes, self.source, self.first, self.rows = routes, source, first, rows
        self.target, self.landed, self.held, self.sems = target, landed, held, sems
        self.number, self.at, self.height = 0, 0, rows
        self.offset, self.offsets, self.pending, self.sent = 0, [], [], []

    def done(self):
        return self.at > 2 * len(self.routes)

    def post(self, source, target, peer):
        copy = send(source, target, self.sems, self.number, peer)
        self.number += 1
        self.pending.append(copy)
        self.sent.append(copy)

    def advance(self):
        if self.done():
            return
        depth = len(self.routes)
        if 1 <= self.at <= depth:
            stage = self.at - 1
            route = self.routes[stage]
            part = self.height // route.size
            total = self.mine[
                pl.ds(pl.multiple_of(self.base + route.index * part, 16), part), :
            ].astype(jnp.float32)
            for step, copy in enumerate(self.pending):
                copy.wait_recv()
                total = total + self.landed[stage][step].astype(jnp.float32)
            self.offset = self.offset + route.index * part
            self.offsets.append(self.offset)
            self.height = part
            if stage < depth - 1:
                self.held[stage][...] = total.astype(jnp.bfloat16)
            else:
                rows = pl.ds(pl.multiple_of(self.first + self.offset, 16), part)
                self.target[rows, :] = total.astype(jnp.bfloat16)
        else:
            for copy in self.pending:
                copy.wait_recv()
            if self.at > depth:
                self.height *= self.routes[2 * depth - self.at].size
        self.pending = []
        if self.at < depth:
            route = self.routes[self.at]
            self.mine, self.base = (
                (self.source, self.first) if self.at == 0 else (self.held[self.at - 1], 0)
            )
            part = self.height // route.size
            for step, (other, peer) in enumerate(zip(route.others, route.peers)):
                rows = pl.ds(pl.multiple_of(self.base + other * part, 16), part)
                self.post(self.mine.at[rows], self.landed[self.at].at[step], peer)
        elif self.at < 2 * depth:
            stage = 2 * depth - 1 - self.at
            first = self.first + self.offsets[stage]
            rows = self.target.at[pl.ds(pl.multiple_of(first, 16), self.height)]
            for peer in self.routes[stage].peers:
                self.post(rows, rows, peer)
        self.at += 1

    def close(self):
        for copy in self.sent:
            copy.wait_send()


def sum_scratch(stages, rows):
    landed, held = [], []
    for stage in stages:
        size = stage_size(stage)
        rows //= size
        landed.append(pltpu.VMEM((max(size - 1, 1), rows, LANES), jnp.bfloat16))
        held.append(pltpu.VMEM((rows, LANES), jnp.bfloat16))
    steps = max(2 * sum(stage_size(stage) - 1 for stage in stages), 1)
    return landed + held + [pltpu.SemaphoreType.DMA((steps, 2))]


def shift_rows(value, amount):
    if amount == 0:
        return value
    row = lax.broadcasted_iota(jnp.int32, value.shape, 0)
    inside = (row + amount >= 0) & (row + amount < TILE)
    return jnp.where(inside, pltpu.roll(value, (-amount) % TILE, 0), 0.0)


def tower_kernel(n_enc, n_dec, tiles, *refs):
    (
        count_ref,
        gap_ref,
        pixels_any,
        stem_any,
        depth_any,
        gain_any,
        up_any,
        down_any,
        layer_any,
        grad_any,
        seq_any,
        big_any,
        little_any,
        pixels_ref,
        stem_ref,
        depth_ref,
        gain_ref,
        up_ref,
        down_ref,
        layer_ref,
        grad_ref,
        info,
        load_sems,
        dec_sems,
        place_ref,
        place_in,
        big_pack,
        little_pack,
        wide,
        rows_in,
        stem_out,
        field,
        taps,
        normed_all,
        act_all,
        proj_all,
        hid_all,
        block_all,
        pool,
        depth_acc,
        small_acc,
        seq_ref,
        big_ref,
        little_ref,
        store_sems,
    ) = refs[:45]
    spare = list(refs[45:])
    enc_here = lax.axis_index("enc")
    dec_here = lax.axis_index("dec")
    span = tiles * TILE
    chunk = 2 * span
    seq = grad_ref.shape[0]
    seq_rows = seq // n_dec

    odd = lax.rem(dec_here, 2)
    ways = [
        [Route(stage, enc_here, dec_here) for stage in big_stages(n_enc, n_dec, turn)]
        for turn in (odd, 1 - odd)
    ]
    little = [Route(stage, enc_here, dec_here) for stage in little_stages(n_enc, n_dec)]
    across = Route([("dec", 1, n_dec)], enc_here, dec_here)

    def take(routes, *rest):
        depth = len(routes)
        landed, held, sems = spare[:depth], spare[depth : 2 * depth], spare[2 * depth]
        del spare[: 2 * depth + 1]
        return Sum(routes, *rest, landed, held, sems)

    sums, ready, first = [], [], 0
    for number, rows in enumerate(chunk_rows(n_enc, n_dec)):
        sums.append(take(ways[number % 2], big_pack, first, rows, big_ref))
        first += rows
        ready.append(first)
    last = take(little, little_pack, 0, little_pack.shape[0], little_ref)

    barrier = pltpu.get_barrier_semaphore()
    greeted = 0
    for route in little:
        for peer in route.peers:
            pl.semaphore_signal(barrier, inc=1, device_id=peer, device_id_type=MESH)
            greeted += 1
    own_rows = pl.ds(pl.multiple_of(dec_here * seq_rows, 16), seq_rows)
    loads = []
    for number, (source, target) in enumerate(
        (
            (pixels_any.at[0], pixels_ref),
            (stem_any, stem_ref),
            (depth_any, depth_ref),
            (gain_any, gain_ref.at[0]),
            (layer_any, layer_ref.at[0]),
            (up_any, up_ref),
            (down_any, down_ref),
            (grad_any.at[0], grad_ref.at[own_rows]),
        )
    ):
        copy = pltpu.make_async_copy(source, target, load_sems.at[number])
        copy.start()
        loads.append(copy)

    count_here = count_ref[0, 0]
    gap_here = gap_ref[0, 0]
    mine = pl.ds(pl.multiple_of(dec_here * 16, 16), 16)
    info[mine, :] = jnp.concatenate(
        [jnp.full((8, LANES), count_here, jnp.int32), jnp.full((8, LANES), gap_here, jnp.int32)],
        axis=0,
    )
    wide[...] = jnp.zeros_like(wide)
    for copy in loads[:3]:
        copy.wait()
    for col in range(TILE):
        wide[col * PATCH_CH : (col + 1) * PATCH_CH, col * WIDTH : (col + 1) * WIDTH] = stem_ref[...]
    for tap in range(KERNEL * KERNEL):
        taps[tap * 8 : tap * 8 + 8, :] = jnp.broadcast_to(
            depth_ref[tap : tap + 1, :].astype(jnp.float32), (8, WIDTH)
        )
    depth_acc[...] = jnp.zeros_like(depth_acc)
    small_acc[...] = jnp.zeros_like(small_acc)
    pix = pixels_ref[...].astype(jnp.float32)
    for tile in range(tiles):
        rows_in[tile * 8 : tile * 8 + 8, :] = jnp.concatenate(
            [pix[tile : tile + 1, r * WIDTH : (r + 1) * WIDTH] for r in range(TILE)], axis=0
        )
    rows = rows_in[...].astype(jnp.bfloat16)
    for col in range(TILE):
        stem_out[col * span : (col + 1) * span, :] = (
            dot(rows, wide[:, col * WIDTH : (col + 1) * WIDTH])
            .astype(jnp.bfloat16)
            .astype(jnp.float32)
        )

    def at(col, tile):
        return pl.ds(pl.multiple_of(col * span + tile * 8, 8), 8)

    def mix(tile, carry):
        for group in range(GROUPS):
            lanes = slice(group * LANES, (group + 1) * LANES)
            source = [stem_out[at(col, tile), lanes] for col in range(TILE)]
            total = [jnp.zeros((8, LANES), jnp.float32)] * TILE
            for a in range(KERNEL):
                moved = [shift_rows(value, a - REACH) for value in source]
                for b in range(KERNEL):
                    tap = a * KERNEL + b
                    weight = taps[tap * 8 : tap * 8 + 8, lanes]
                    for col in range(TILE):
                        other = col + b - REACH
                        if 0 <= other < TILE:
                            total[col] = total[col] + moved[other] * weight
            for col in range(TILE):
                field[at(col, tile), lanes] = total[col]
        return carry

    part = tiles * 2 // 3
    lax.fori_loop(0, part, mix, 0)
    pl.semaphore_wait(barrier, greeted)
    copies = []
    for step, peer in enumerate(across.peers):
        copies.append(send(info.at[mine], info.at[mine], dec_sems, 3 * step, peer))
        copies.append(send(grad_any.at[0], grad_ref.at[own_rows], dec_sems, 3 * step + 1, peer))
    lax.fori_loop(part, tiles, mix, 0)
    for copy in loads[3:]:
        copy.wait()
    for copy in copies:
        copy.wait()

    start = jnp.full((8, LANES), gap_here, jnp.int32)
    for other in range(n_dec):
        gone = info[other * 16 : other * 16 + 8, :] * FEAT_TILE
        gone = gone + info[other * 16 + 8 : other * 16 + 16, :]
        start = start + jnp.where(other < dec_here, gone, 0)
    start = start[0:1, 0:1]
    count = info[mine, :][0:1, 0:1]
    gain = gain_ref[...]
    layer = layer_ref[...]

    def fold(value):
        return jnp.sum(value.reshape(-1, 8, WIDTH), axis=0)

    def block(pair, carry):
        here = pl.ds(pl.multiple_of(pair * chunk, 16), chunk)
        mixed = field[here, :]
        dev = mixed - jnp.mean(mixed, axis=1, keepdims=True)
        inv = lax.rsqrt(jnp.mean(dev * dev, axis=1, keepdims=True) + EPSILON)
        centred = dev * inv
        normed = (centred * gain).astype(jnp.bfloat16)
        normed_all[here, :] = normed
        hidden = dot(normed, up_ref[...])
        square = hidden * hidden
        half = 0.5 + 0.5 * jnp.tanh(GELU_A * hidden * (1.0 + GELU_B * square))
        act = (hidden * half).astype(jnp.bfloat16)
        slope = half + hidden * (2.0 * half * (1.0 - half)) * (
            GELU_A + (3.0 * GELU_A * GELU_B) * square
        )
        act_all[here, :] = act
        projected = dot(act, down_ref[...])
        out = stem_out[here, :] + layer * projected
        both = out[:span] + out[span:]
        both = both + pltpu.roll(both, span - 1, 0)
        pool[pl.ds(pl.multiple_of(pair * span, 8), span), :] = 0.25 * both

        row = lax.broadcasted_iota(jnp.int32, (span, seq), 0)
        spot = lax.broadcasted_iota(jnp.int32, (span, seq), 1)
        tile = row // TILE
        want = start + tile * FEAT_TILE + (row % TILE) // 2 * 4 + pair
        pick = jnp.where((spot == want) & (tile < count), 0.25, 0.0).astype(jnp.bfloat16)
        once = dot(pick, grad_ref[...])
        grad_block = jnp.concatenate([once, once], axis=0)
        block_all[here, :] = grad_block
        small_acc[0:8, :] += fold(grad_block * projected)
        grad_proj = (grad_block * layer).astype(jnp.bfloat16)
        proj_all[here, :] = grad_proj
        grad_act = dot(grad_proj, down_ref[...], NT)
        grad_hidden = (grad_act * slope).astype(jnp.bfloat16)
        hid_all[here, :] = grad_hidden
        grad_normed = dot(grad_hidden, up_ref[...], NT)
        small_acc[8:16, :] += fold(grad_normed * centred)
        scaled = grad_normed * gain
        field[here, :] = inv * (
            scaled
            - jnp.mean(scaled, axis=1, keepdims=True)
            - centred * jnp.mean(scaled * centred, axis=1, keepdims=True)
        )
        return carry

    lax.fori_loop(0, TILE // 2, block, 0)

    def pack(target, first, value):
        height = value.shape[0]
        for group in range(value.shape[1] // LANES):
            at_row = first + group * height
            target[at_row : at_row + height, :] = value[
                :, group * LANES : (group + 1) * LANES
            ].astype(jnp.bfloat16)

    def begin(filled):
        for one, end in zip(sums, ready):
            if one.at == 0 and (end <= filled or filled == BIG):
                one.advance()

    def advance(ones):
        for one in ones:
            one.advance()

    if big_pack.shape[0] > BIG:
        big_pack[BIG:, :] = jnp.zeros((big_pack.shape[0] - BIG, LANES), jnp.bfloat16)
    normed_t = normed_all[...].T
    pack(big_pack, UP_AT, dot(normed_t, hid_all[:, :WIDTH]))
    begin(DOWN_AT // 2)
    pack(big_pack, DOWN_AT // 2, dot(normed_t, hid_all[:, WIDTH:]))
    begin(DOWN_AT)
    early = [one for one in sums if one.at > 0]
    pack(big_pack, DOWN_AT, dot(act_all[...], proj_all[...], TN))
    begin(BIG)
    advance(early)

    place = jnp.zeros((seq, WIDTH), jnp.float32)
    for pair in range(TILE // 2):
        spot = lax.broadcasted_iota(jnp.int32, (seq, span), 0)
        row = lax.broadcasted_iota(jnp.int32, (seq, span), 1)
        tile = row // TILE
        want = start + tile * FEAT_TILE + (row % TILE) // 2 * 4 + pair
        hit = (spot == want) & (tile < count) & (row % 2 == 0)
        place = place + dot(
            jnp.where(hit, 1.0, 0.0).astype(jnp.bfloat16),
            pool[pair * span : (pair + 1) * span, :].astype(jnp.bfloat16),
        )
    place_ref[...] = place.astype(jnp.bfloat16)

    places = []
    for step, (other, peer) in enumerate(zip(across.others, across.peers)):
        rows_to = pl.ds(pl.multiple_of(other * seq_rows, 16), seq_rows)
        places.append(send(place_ref.at[rows_to], place_in.at[step], dec_sems, 3 * step + 2, peer))

    def unmix(tile, carry):
        for group in range(GROUPS):
            lanes = slice(group * LANES, (group + 1) * LANES)
            grads = [field[at(col, tile), lanes] for col in range(TILE)]
            source = [stem_out[at(col, tile), lanes] for col in range(TILE)]
            total = [block_all[at(col, tile), lanes] for col in range(TILE)]
            for a in range(KERNEL):
                moved = [shift_rows(value, REACH - a) for value in grads]
                for b in range(KERNEL):
                    tap = a * KERNEL + b
                    weight = taps[tap * 8 : tap * 8 + 8, lanes]
                    term = None
                    for col in range(TILE):
                        other = col - b + REACH
                        if 0 <= other < TILE:
                            total[col] = total[col] + moved[other] * weight
                            product = moved[other] * source[col]
                            term = product if term is None else term + product
                    depth_acc[tap * 8 : tap * 8 + 8, lanes] += term
            for col in range(TILE):
                block_all[at(col, tile), lanes] = total[col]
        return carry

    for third in range(3):
        lax.fori_loop(tiles * third // 3, tiles * (third + 1) // 3, unmix, 0)
        advance(sums)

    stem_term = jnp.zeros((PATCH_CH, WIDTH), jnp.float32)
    for col in range(TILE):
        grad_stem = block_all[col * span : (col + 1) * span, :].astype(jnp.bfloat16)
        stem_term = (
            stem_term + dot(rows, grad_stem, TN)[col * PATCH_CH : (col + 1) * PATCH_CH, :]
        )
    pack(little_pack, STEM_AT, stem_term)
    taps_sum = jnp.sum(depth_acc[...].reshape(KERNEL * KERNEL, 8, WIDTH), axis=1)
    small = jnp.concatenate(
        [
            taps_sum,
            jnp.zeros((GAIN_ROW - KERNEL * KERNEL, WIDTH), jnp.float32),
            jnp.sum(small_acc[8:16, :], axis=0, keepdims=True),
            jnp.sum(small_acc[0:8, :], axis=0, keepdims=True),
            jnp.zeros((SMALL - SCALE_ROW - 1, WIDTH), jnp.float32),
        ],
        axis=0,
    )
    pack(little_pack, SMALL_AT, small)
    if little_pack.shape[0] > LITTLE:
        little_pack[LITTLE:, :] = jnp.zeros((little_pack.shape[0] - LITTLE, LANES), jnp.bfloat16)
    last.advance()

    sequence = place_ref[own_rows, :].astype(jnp.float32)
    for step, copy in enumerate(places):
        copy.wait_recv()
        sequence = sequence + place_in[step].astype(jnp.float32)
    seq_ref[...] = sequence.astype(jnp.bfloat16)
    stores = []

    def store(source, target):
        copy = pltpu.make_async_copy(source, target, store_sems.at[len(stores)])
        copy.start()
        stores.append(copy)

    store(seq_ref, seq_any)
    while not (last.done() and all(one.done() for one in sums)):
        for one, end in zip(sums, ready):
            if not one.done():
                one.advance()
                if one.done():
                    rows = slice(one.first, end)
                    store(big_ref.at[rows], big_any.at[rows])
        if not last.done():
            last.advance()
            if last.done():
                store(little_ref, little_any)
    for one in [*sums, last]:
        one.close()
    for copy in stores:
        copy.wait()
    for copy in places:
        copy.wait_send()


def tower(n_enc, n_dec, args):
    pixels, grad = args[2], args[-1]
    tiles = pixels.shape[1]
    positions = tiles * TILE * TILE
    span = tiles * TILE
    seq_rows = grad.shape[1]
    seq = n_dec * seq_rows
    f32, bf16 = jnp.float32, jnp.bfloat16
    chunks = chunk_rows(n_enc, n_dec)
    big_rows = sum(chunks)
    unit = n_enc * n_dec * 16
    little_rows = -(-LITTLE // unit) * unit
    steps = max(n_dec - 1, 1)
    smem = pl.BlockSpec(memory_space=pltpu.SMEM)
    scratch = [
        pltpu.VMEM((tiles, TILE * TILE * PATCH_CH), bf16),
        pltpu.VMEM((PATCH_CH, WIDTH), bf16),
        pltpu.VMEM((KERNEL * KERNEL, WIDTH), bf16),
        pltpu.VMEM((1, WIDTH), f32),
        pltpu.VMEM((WIDTH, INNER), bf16),
        pltpu.VMEM((INNER, WIDTH), bf16),
        pltpu.VMEM((1, WIDTH), f32),
        pltpu.VMEM((seq, WIDTH), bf16),
        pltpu.VMEM((n_dec * 16, LANES), jnp.int32),
        pltpu.SemaphoreType.DMA((8,)),
        pltpu.SemaphoreType.DMA((3 * steps, 2)),
        pltpu.VMEM((seq, WIDTH), bf16),
        pltpu.VMEM((steps, seq_rows, WIDTH), bf16),
        pltpu.VMEM((big_rows, LANES), bf16),
        pltpu.VMEM((little_rows, LANES), bf16),
        pltpu.VMEM((WIDTH, TILE * WIDTH), bf16),
        pltpu.VMEM((span, WIDTH), f32),
        pltpu.VMEM((positions, WIDTH), f32),
        pltpu.VMEM((positions, WIDTH), f32),
        pltpu.VMEM((KERNEL * KERNEL * 8, WIDTH), f32),
        pltpu.VMEM((positions, WIDTH), bf16),
        pltpu.VMEM((positions, INNER), bf16),
        pltpu.VMEM((positions, WIDTH), bf16),
        pltpu.VMEM((positions, INNER), bf16),
        pltpu.VMEM((positions, WIDTH), f32),
        pltpu.VMEM((positions // 2, WIDTH), f32),
        pltpu.VMEM((KERNEL * KERNEL * 8, WIDTH), f32),
        pltpu.VMEM((16, WIDTH), f32),
        pltpu.VMEM((seq_rows, WIDTH), bf16),
        pltpu.VMEM((big_rows, LANES), bf16),
        pltpu.VMEM((little_rows, LANES), bf16),
        pltpu.SemaphoreType.DMA((len(chunks) + 2,)),
    ]
    for rows in chunks:
        scratch += sum_scratch(big_stages(n_enc, n_dec), rows)
    scratch += sum_scratch(little_stages(n_enc, n_dec), little_rows)
    return pl.pallas_call(
        functools.partial(tower_kernel, n_enc, n_dec, tiles),
        out_shape=(
            jax.ShapeDtypeStruct((seq_rows, WIDTH), bf16),
            jax.ShapeDtypeStruct((big_rows, LANES), bf16),
            jax.ShapeDtypeStruct((little_rows, LANES), bf16),
        ),
        in_specs=[smem, smem] + [whole_ref()] * 8,
        out_specs=(whole_ref(),) * 3,
        scratch_shapes=scratch,
        compiler_params=pltpu.CompilerParams(
            collective_id=0, has_side_effects=True, vmem_limit_bytes=56 * 2**20
        ),
        name="tower",
    )(*args)


def unpack_kernel(scale, seq_any, big_any, little_any, *refs):
    outs, holds, sems = refs[:7], refs[7:14], refs[14]
    big, little = refs[15:]
    seq_ref, stem_ref, depth_ref, gain_ref, up_ref, down_ref, scale_ref = holds
    copies, loads = [], []
    for number, (source, target) in enumerate(
        (
            (big_any.at[UP_AT:DOWN_AT], big.at[UP_AT:DOWN_AT]),
            (big_any.at[DOWN_AT:BIG], big.at[DOWN_AT:BIG]),
            (seq_any, seq_ref),
            (little_any, little),
        )
    ):
        copy = pltpu.make_async_copy(source, target, sems.at[number])
        copy.start()
        loads.append(copy)

    def store(number, rows=None):
        source, target = holds[number], outs[number]
        if number == 0:
            target = target.at[0]
        if number in (3, 6):
            source = source.at[0]
        if rows is not None:
            source, target = source.at[rows], target.at[rows]
        copy = pltpu.make_async_copy(source, target, sems.at[4 + len(copies)])
        copy.start()
        copies.append(copy)

    def unpack(source, first, rows, group):
        at_row = first + group * rows
        return source[at_row : at_row + rows, :].astype(jnp.float32) * scale

    def halves(number, first, rows, groups):
        part = rows // 2
        for half in range(2):
            here = slice(half * part, (half + 1) * part)
            for group in range(groups):
                at_row = first + group * rows + half * part
                holds[number][here, group * LANES : (group + 1) * LANES] = unpack(
                    big, at_row, part, 0
                )
            store(number, here)

    loads[0].wait()
    halves(4, UP_AT, WIDTH, INNER // LANES)
    loads[1].wait()
    halves(5, DOWN_AT, INNER, GROUPS)
    loads[2].wait()
    store(0)
    loads[3].wait()
    for group in range(GROUPS):
        lanes = slice(group * LANES, (group + 1) * LANES)
        stem_ref[:, lanes] = unpack(little, STEM_AT, PATCH_CH, group)
        small = unpack(little, SMALL_AT, SMALL, group)
        depth_ref[:, lanes] = small[: KERNEL * KERNEL]
        gain_ref[:, lanes] = small[GAIN_ROW : GAIN_ROW + 1]
        scale_ref[:, lanes] = small[SCALE_ROW : SCALE_ROW + 1]
    for number in (1, 2, 3, 6):
        store(number)
    for copy in copies:
        copy.wait()


def unpack_all(scale, sequence, big, little):
    f32, bf16 = jnp.float32, jnp.bfloat16
    seq_rows = sequence.shape[0]
    shapes = [
        ((1, seq_rows, WIDTH), bf16),
        ((PATCH_CH, WIDTH), f32),
        ((KERNEL * KERNEL, WIDTH), f32),
        ((WIDTH,), f32),
        ((WIDTH, INNER), f32),
        ((INNER, WIDTH), f32),
        ((WIDTH,), f32),
    ]
    held = [(seq_rows, WIDTH)] + [s if len(s) == 2 else (1, WIDTH) for s, _ in shapes[1:]]
    return pl.pallas_call(
        functools.partial(unpack_kernel, scale),
        out_shape=tuple(jax.ShapeDtypeStruct(s, kind) for s, kind in shapes),
        in_specs=[pl.BlockSpec(memory_space=pltpu.HBM)] * 3,
        out_specs=(whole_ref(),) * 7,
        scratch_shapes=[pltpu.VMEM(s, kind) for s, (_, kind) in zip(held, shapes)]
        + [
            pltpu.SemaphoreType.DMA((24,)),
            pltpu.VMEM(big.shape, bf16),
            pltpu.VMEM(little.shape, bf16),
        ],
        compiler_params=pltpu.CompilerParams(vmem_limit_bytes=56 * 2**20),
        name="unpack",
    )(sequence, big, little)


def on_device(
    pixels,
    tile_counts,
    text_gaps,
    stem_weight,
    depth_weight,
    norm_gain,
    up_weight,
    down_weight,
    layer_scale,
    embed_grad,
):
    n_enc = lax.axis_size("enc")
    n_dec = lax.axis_size("dec")
    weights = (stem_weight, depth_weight, norm_gain, up_weight, down_weight, layer_scale)
    sequence, big, little = tower(
        n_enc, n_dec, (tile_counts, text_gaps, pixels, *weights, embed_grad)
    )
    scale = 1.0 / math.sqrt(n_dec * n_enc * MEAN_TILES * FEAT_TILE)
    return unpack_all(scale, sequence, big, little)


def solution(mesh):
    return jax.shard_map(
        on_device,
        mesh=mesh,
        in_specs=(
            P("dec", "enc", None),
            P("dec", "enc"),
            P("dec", "enc"),
            P(),
            P(),
            P(),
            P(),
            P(),
            P(),
            P("enc", "dec", None),
        ),
        out_specs=(P("enc", "dec", None), P(), P(), P(), P(), P(), P()),
        check_vma=False,
    )
```
